128 devices in a mesh: ts: 8 (over x_hi, z), dp: 2 (over x_lo), ep: 8 (over y, core).
Axes of the slice: x: 4 (x_hi: 2, x_lo: 2; x = x_hi * 2 + x_lo), y: 4, z: 4, core: 2. Of those that a mesh axis runs over, the one named last changes fastest.
Arguments:
- tokens: bfloat16 [64, 128, 2560], P(('ts', 'ep'), 'dp'), may hold values from -6 to 6
- out_grad: bfloat16 [64, 128, 2560], P(('ts', 'ep'), 'dp'), may hold values from -6 to 6
- routes: int32 [64, 128, 6], P(('ts', 'ep')), may hold values from 0 to 63, all different within a row; in each aligned block of 64 rows (0 to 63, 64 to 127, ..., all dimensions but the last counted through in order) at most 9 rows name the same one
- norm_gain: bfloat16 [2560], replicated, may hold values from 0.099609375 to 1.8984375
- router_w: bfloat16 [2560, 64], replicated, may hold values from -0.125 to 0.125
- w_gate: bfloat16 [64, 1536, 2560], P(('ts', 'ep'), 'dp'), may hold values from -0.125 to 0.125
- w_up: bfloat16 [64, 1536, 2560], P(('ts', 'ep'), 'dp'), may hold values from -0.125 to 0.125
- w_down: bfloat16 [64, 1536, 2560], P(('ts', 'ep'), 'dp'), may hold values from -0.15625 to 0.15625
Outputs:
- grad_x: float32 [64, 128, 2560], P(('ts', 'ep'), 'dp')
- grad_gate: bfloat16 [64, 1536, 2560], P(('ts', 'ep'), 'dp')
- grad_up: bfloat16 [64, 1536, 2560], P(('ts', 'ep'), 'dp')
- grad_down: bfloat16 [64, 1536, 2560], P(('ts', 'ep'), 'dp')
- grad_router: float32 [2560, 64], replicated
- grad_gain: float32 [2560], replicated
The draws below stay inside these ranges and needn't reach their ends.
Inputs may be any that keep to these rules, and one draw needn't show every extreme that they name: `routes`: each row names 6 different experts; in the rows of one device (aligned blocks of 64 rows) no expert is named more than 9 times, a bound that some block reaches.
All inputs are finite; a program needn't handle non-finite values.
Results may differ from the reference program's by a relative error of at most 0.0079.
Values may be sent and summed in bfloat16 or wider, within the bound.
A program may use at most 192 MiB of HBM per device.

```python
import math
import jax
import jax.numpy as jnp
import numpy as np
from jax import lax

D = 2560
FF = 1536
TOP = 6
TOK_DEV = 64
GROUPS = 64
TOK_GROUP = 128
TOKENS = 8192
EXPERTS = 64
MOST = 9
CAP = 18


def steps_of(rng, shape, split, smallest, top_value):
    def one(position, shards_of):
        steps = jax.random.uniform(jax.random.fold_in(jax.random.fold_in(rng, 6), position), (shards_of,), jnp.float32, smallest / len(split), top_value / len(split))
        return jnp.repeat(jnp.exp(steps), shape[position] // shards_of).reshape((-1,) + (1,) * (len(shape) - position - 1))

    loudness = one(*split[0])
    for cut in split[1:]:
        loudness = loudness * one(*cut)
    return loudness


def deal_out(key, own, number, rows, number_of, top, most, lean):
    order = jax.random.permutation(key, number_of)
    crowded, common = portions_of(number_of, rows * top, most, lean, True), portions_of(number_of, rows * top, most, lean, False)
    places = jnp.arange(number_of)

    def named(tallies, offset_by):
        used = int((tallies > 0).sum())
        fixed = max(1, used // 4)
        shifted = fixed + (places - fixed + offset_by * (used - fixed)) % max(1, number_of - fixed)
        return jnp.zeros((number_of,), jnp.int32).at[order[jnp.where(places < fixed, places, shifted)]].set(jnp.asarray(tallies, jnp.int32))

    tallies = jnp.where(number % 4 == 0, named(crowded, number // 4), named(common, number - number // 4 - 1))
    mixed = jax.random.permutation(jax.random.fold_in(own, 3), number_of)
    giver, receiver = mixed[0:number_of // 2 * 2:2], mixed[1:number_of // 2 * 2:2]
    room = jnp.minimum(tallies[giver] - 1, most - tallies[receiver]) // 2
    room = jnp.where((giver == order[0]) | (receiver == order[0]) | (tallies[receiver] == 0), 0, jnp.maximum(room, 0))
    shifted = jax.random.randint(jax.random.fold_in(own, 4), (number_of // 2,), 0, 1 << 20) % (room + 1)
    tallies = tallies.at[giver].add(-shifted).at[receiver].add(shifted)
    items = jnp.searchsorted(jnp.cumsum(tallies), jnp.arange(rows * top), side="right").astype(jnp.int32)
    grid = items.reshape(top, rows).T
    grid = grid[jax.random.permutation(jax.random.fold_in(own, 1), rows)]
    offset_by = jax.random.randint(jax.random.fold_in(own, 2), (rows, 1), 0, top)
    return jnp.take_along_axis(grid, (jnp.arange(top)[None, :] + offset_by) % top, axis=1)


def portions_of(count, total, most, skew, full):
    weights = [(1 << 20) // math.isqrt(rank ** skew) + 1 for rank in range(1, count + 1)]
    largest = most if full else min(most, max(-(-total // count), total * weights[0] // sum(weights)))
    least = 1 if total - largest >= count - 1 else 0
    counts, surplus = [largest] + [least] * (count - 1), total - largest - least * (count - 1)
    while surplus > 0:
        free = [i for i in range(1, count) if counts[i] < largest] or [i for i in range(1, count) if counts[i] < most]
        whole, left = sum([weights[i] for i in free]), surplus
        for i in free:
            addition = min(most - counts[i], max(1, left * weights[i] // whole), surplus)
            counts[i] = counts[i] + addition
            surplus = surplus - addition
    return np.array(counts)


def bell_draw(own_key, shape, spread, most, split=(), kind=jnp.bfloat16):
    values = spread * jax.random.normal(own_key, shape, jnp.float32)
    if split:
        values = values * steps_of(own_key, shape, split, -0.22, 0.18)
    return jnp.clip(values, -most, most).astype(kind)


def setup_inputs(seed: int = 0) -> dict:
    streams_of = jax.random.split(jax.random.key(seed), 9)
    tokens = bell_draw(streams_of[0], (GROUPS, TOK_GROUP, D), 1.0, 6.0, ((0, 64), (1, 2)))
    out_grad = bell_draw(streams_of[1], (GROUPS, TOK_GROUP, D), 1.0, 6.0, ((0, 64), (1, 2)))
    routes_keys = jax.random.split(jax.random.fold_in(streams_of[2], 1), GROUPS * TOK_GROUP // TOK_DEV)
    routes_turns = jax.random.permutation(jax.random.fold_in(streams_of[2], 3), GROUPS * TOK_GROUP // TOK_DEV)
    routes = jax.vmap(lambda own, number: deal_out(jax.random.fold_in(streams_of[2], 2), own, number, TOK_DEV, EXPERTS, TOP, MOST, 2))(routes_keys, routes_turns).reshape((GROUPS, TOK_GROUP, TOP))
    norm_gain = jnp.clip(1.0 + 0.18 * jax.random.normal(streams_of[3], (D,), jnp.float32), 0.099609375, 1.8984375).astype(jnp.bfloat16)
    router_w = bell_draw(streams_of[4], (D, EXPERTS), D ** -0.5, 0.125)
    w_gate = bell_draw(streams_of[5], (EXPERTS, FF, D), D ** -0.5, 0.125, ((0, 64), (1, 2)))
    w_up = bell_draw(streams_of[6], (EXPERTS, FF, D), D ** -0.5, 0.125, ((0, 64), (1, 2)))
    w_down = bell_draw(streams_of[7], (EXPERTS, FF, D), FF ** -0.5, 0.15625, ((0, 64), (1, 2)))
    return dict(tokens=tokens, out_grad=out_grad, routes=routes, norm_gain=norm_gain, router_w=router_w, w_gate=w_gate, w_up=w_up, w_down=w_down)


def norm_parts(inputs, norm_gain):
    widened = inputs.astype(jnp.float32)
    inv_scale = lax.rsqrt(lax.optimization_barrier(jnp.mean(widened * widened, axis=-1, keepdims=True)) + 1e-06)
    normed = widened * inv_scale
    return ((normed * norm_gain.astype(jnp.float32)).astype(jnp.bfloat16), normed, inv_scale)

def reference(tokens, out_grad, routes, norm_gain, router_w, w_gate, w_up, w_down):
    inputs = tokens.reshape(TOKENS, D)
    grad_out = out_grad.reshape(TOKENS, D)
    chosen_ids = routes.reshape(TOKENS, TOP)
    normed_u, normed_v, inv_scale = norm_parts(inputs, norm_gain)
    logits = jnp.dot(normed_u, router_w, preferred_element_type=jnp.float32)
    affinity = jax.nn.sigmoid(logits)
    picked = jnp.take_along_axis(affinity, chosen_ids, axis=1)
    totals = lax.optimization_barrier(jnp.sum(picked, axis=1, keepdims=True))
    gate_values = picked / totals
    gate_wire = gate_values.astype(jnp.bfloat16)
    capacity = GROUPS * CAP
    positions = jnp.arange(capacity, dtype=jnp.int32)

    def per_expert(carry, layer):
        row_total, dot_total = carry
        gate_w, up_w, down_w, expert = layer
        hits = chosen_ids == expert
        member = jnp.any(hits, axis=1)
        count = jnp.sum(member.astype(jnp.int32))
        index = jnp.nonzero(member, size=capacity, fill_value=0)[0].astype(jnp.int32)
        valid = positions < count
        weight_in = lax.optimization_barrier(jnp.sum(jnp.where(hits, gate_wire.astype(jnp.float32), 0.0), axis=1)).astype(jnp.bfloat16)
        sel_u = jnp.where(valid[:, None], normed_u[index], jnp.zeros_like(normed_u[index]))
        sel_dy = jnp.where(valid[:, None], grad_out[index], jnp.zeros_like(grad_out[index]))
        sel_g = jnp.where(valid, weight_in[index], jnp.zeros_like(weight_in[index]))
        pre_gate = jnp.dot(sel_u, gate_w.T, preferred_element_type=jnp.float32)
        pre_up = jnp.dot(sel_u, up_w.T, preferred_element_type=jnp.float32)
        active = jax.nn.silu(pre_gate)
        hidden = (active * pre_up).astype(jnp.bfloat16)
        output = jnp.dot(hidden, down_w, preferred_element_type=jnp.float32)
        gate_dots = lax.optimization_barrier(jnp.sum(sel_dy.astype(jnp.float32) * output, axis=-1))
        scaled_grad = (sel_g.astype(jnp.float32)[:, None] * sel_dy.astype(jnp.float32)).astype(jnp.bfloat16)
        hidden_grad = jnp.dot(scaled_grad, down_w.T, preferred_element_type=jnp.float32)
        sigma = jax.nn.sigmoid(pre_gate)
        gate_grad = (hidden_grad * pre_up * sigma * (1.0 + pre_gate * (1.0 - sigma))).astype(jnp.bfloat16)
        up_grad = (hidden_grad * active).astype(jnp.bfloat16)
        grad_down = jnp.dot(hidden.T, scaled_grad, preferred_element_type=jnp.float32).astype(jnp.bfloat16)
        grad_gate = jnp.dot(gate_grad.T, sel_u, preferred_element_type=jnp.float32).astype(jnp.bfloat16)
        grad_up = jnp.dot(up_grad.T, sel_u, preferred_element_type=jnp.float32).astype(jnp.bfloat16)
        row_grads = jnp.dot(gate_grad, gate_w, preferred_element_type=jnp.float32)
        row_grads = row_grads + jnp.dot(up_grad, up_w, preferred_element_type=jnp.float32)
        row_total = row_total.at[index].add(jnp.where(valid[:, None], row_grads, 0.0))
        dot_part = hits[index].astype(jnp.float32) * gate_dots[:, None]
        dot_total = dot_total.at[index].add(jnp.where(valid[:, None], dot_part, 0.0))
        return ((row_total, dot_total), (grad_gate, grad_up, grad_down))
    start = (jnp.zeros((TOKENS, D), jnp.float32), jnp.zeros((TOKENS, TOP), jnp.float32))
    layers = (w_gate, w_up, w_down, jnp.arange(EXPERTS, dtype=jnp.int32))
    (expert_part, gate_dots), (grad_gate, grad_up, grad_down) = lax.scan(per_expert, start, layers)
    mixed = lax.optimization_barrier(jnp.sum(gate_values * gate_dots, axis=1, keepdims=True))
    steer = (gate_dots - mixed) / totals
    onehot = (chosen_ids[:, :, None] == jnp.arange(EXPERTS, dtype=jnp.int32)[None, None, :]).astype(jnp.float32)
    dlogits = lax.optimization_barrier(jnp.sum(onehot * steer[:, :, None], axis=1)) * affinity * (1.0 - affinity)
    router_wide = router_w.astype(jnp.float32)
    row_grad = expert_part + jnp.dot(dlogits, router_wide.T, precision=lax.Precision.HIGHEST)
    grad_router = jnp.dot(normed_u.astype(jnp.float32).T, dlogits, precision=lax.Precision.HIGHEST)
    scaled = row_grad * norm_gain.astype(jnp.float32)
    grad_x = inv_scale * scaled - normed_v * inv_scale * lax.optimization_barrier(jnp.mean(normed_v * scaled, axis=-1, keepdims=True))
    grad_gain = lax.optimization_barrier(jnp.sum(row_grad * normed_v, axis=0))
    return (grad_x.reshape(GROUPS, TOK_GROUP, D), grad_gate, grad_up, grad_down, grad_router, grad_gain)
```

```python
import jax
import jax.numpy as jnp
from jax import lax
from jax.experimental import pallas as pl
from jax.experimental.pallas import tpu as pltpu
from jax.sharding import PartitionSpec as P

MESH = pl.DeviceIdType.MESH
F32 = jnp.float32
BF16 = jnp.bfloat16
D = 2560
NC = 4
CW = D // NC
TOK = 64
MOST = 9
SRC = 16
MSG = SRC * MOST
PEERS = 8
ROWS = PEERS * MSG
ALL = SRC * TOK
SH = 768
EXPERTS = 64
KA = 640
KB = ROWS - KA
NT = (((1,), (1,)), ((), ()))
TN = (((0,), (0,)), ((), ()))


def dot(a, b, dims=(((1,), (0,)), ((), ()))):
    return lax.dot_general(a, b, dims, preferred_element_type=F32)


def split(a):
    hi = a.astype(BF16)
    return hi, (a - hi.astype(F32)).astype(BF16)


def kernel(
    tok, dy, rt, gain, rwt, wg_in, wu_in, wd_in,
    gx_out, gr_out, gn_out, gg_out, gu_out, gd_out,
    xall, rall, send, wg, wu, wd, acc1, acc2, q, s, h, da, db, pk,
    rts, zt, slots, gs, gr, ds_, dr, dgt, dgr, gwrow, dgrow, rowg, dzs, gaccum,
    wsem, osem, lsem,
    rt_ss, rt_rs, a_ss, a_rs, b_ss, b_rs, d_ss, d_rs, g_ss, g_rs, dg_ss, dg_rs, dt_ss, dt_rs,
    r_ss, r_rs, z_ss, z_rs, x_ss, x_rs, free_sem,
):
    ts, dp, ep = lax.axis_index("ts"), lax.axis_index("dp"), lax.axis_index("ep")
    xh, z = ts // 4, ts % 4
    x = xh * 2 + dp
    y, core = ep // 2, ep % 2
    me = z * 4 + x

    def at_xz(zz, xx):
        return ((xx // 2) * 4 + zz, xx % 2, ep)

    def at_ep(e):
        return (ts, dp, e)

    def remote(src, dst, ss, rs, dev):
        return pltpu.make_async_remote_copy(
            src_ref=src, dst_ref=dst, send_sem=ss, recv_sem=rs, device_id=dev, device_id_type=MESH
        )

    def wcopy(i, c):
        src, dst = ((wg_in, wg), (wu_in, wu), (wd_in, wd))[i]
        return pltpu.make_async_copy(src.at[:, pl.ds(c * CW, CW)], dst.at[c], wsem.at[i, c])

    for c in range(NC):
        for i in range(3):
            wcopy(i, c).start()

    barrier = pltpu.get_barrier_semaphore()
    for i in range(1, PEERS):
        pl.semaphore_signal(barrier, inc=1, device_id=at_ep((ep + i) % PEERS), device_id_type=MESH)
    for i in range(1, SRC):
        p = (me + i) % SRC
        pl.semaphore_signal(barrier, inc=1, device_id=at_xz(p // 4, p % 4), device_id_type=MESH)
    pl.semaphore_wait(barrier, PEERS - 1 + SRC - 1)

    myb = z * 2 + xh
    rts[myb] = rt[...]

    def rt_copy(i):
        t = (ts + i) % 8
        return remote(rt, rts.at[myb], rt_ss.at[i - 1], rt_rs.at[i - 1], (t, dp, ep))

    for i in range(1, 8):
        rt_copy(i).start()

    mine = pl.multiple_of(me * TOK, TOK)
    wide = tok[...].astype(F32)
    inv = lax.rsqrt(jnp.mean(wide * wide, axis=1, keepdims=True) + 1e-06)
    u_own = (wide * inv * gain[...]).astype(BF16)
    for c in range(NC):
        xall[c, pl.ds(mine, TOK), :] = u_own[:, c * CW : (c + 1) * CW]
        xall[NC + c, pl.ds(mine, TOK), :] = dy[:, c * CW : (c + 1) * CW]

    def a_copy(st, i):
        block = xall.at[st, pl.ds(mine, TOK)]
        return remote(block, block, a_ss.at[st, i - 1], a_rs.at[st, i - 1], at_xz(z, (x + i) % 4))

    line = pl.multiple_of(z * 4 * TOK, 4 * TOK)

    def b_copy(st, i):
        block = xall.at[st, pl.ds(line, 4 * TOK)]
        return remote(block, block, b_ss.at[st, i - 1], b_rs.at[st, i - 1], at_xz((z + i) % 4, x))

    for st in range(2 * NC):
        for i in (1, 3, 2):
            a_copy(st, i).start()

    def forward(st):
        for i in (1, 3, 2):
            a_copy(st, i).wait_recv()
        for i in (1, 3, 2):
            b_copy(st, i).start()

    forward(0)
    forward(1)

    for i in range(1, 8):
        rt_copy(i).wait_recv()
    lane = lax.broadcasted_iota(jnp.int32, (128, 128), 1)
    sub = lax.broadcasted_iota(jnp.int32, (128, 128), 0)
    before = jnp.where((sub < lane) & ((sub // TOK) == (lane // TOK)), 1.0, 0.0).astype(BF16)
    for b in range(8):
        r = rts[b]
        ids = lax.broadcasted_iota(jnp.int32, (16, 128), 0)
        own = jnp.zeros((16, 128), F32)
        for k in range(6):
            own = own + jnp.where((r[k : k + 1, :] == ts * PEERS + ids) & (ids < PEERS), 1.0, 0.0)
        rank = dot(own.astype(BF16), before)
        half = lax.broadcasted_iota(jnp.int32, (16, 128), 1) // TOK
        slot = jnp.where(own > 0.5, (2 * b + half) * MOST + rank.astype(jnp.int32), -1)
        slots[:, b * 128 : (b + 1) * 128] = slot

    def slot_body(d, _):
        row = slots[pl.ds(d, 1), :]
        hit = lax.broadcasted_iota(jnp.int32, (MSG, ALL), 0) == row
        pk[pl.ds(pl.multiple_of(d * MSG, MSG), MSG), :] = jnp.where(hit, 1.0, 0.0).astype(BF16)
        return 0

    lax.fori_loop(0, PEERS, slot_body, 0)
    def d_copy(st, i):
        e = (ep + i) % PEERS
        return remote(
            send.at[st % NC, pl.ds(pl.multiple_of(e * MSG, MSG), MSG)],
            rall.at[st, pl.ds(pl.multiple_of(ep * MSG, MSG), MSG)],
            d_ss.at[st, i - 1],
            d_rs.at[st, i - 1],
            at_ep(e),
        )

    own_rows = pl.ds(pl.multiple_of(ep * MSG, MSG), MSG)

    def own_copy(st):
        return pltpu.make_async_copy(send.at[st % NC, own_rows], rall.at[st, own_rows], lsem.at[st])

    def pack(st):
        for i in (1, 3, 2):
            b_copy(st, i).wait_recv()

        def body(i, _):
            yy = (y + 1 + i) % 4
            rows = pl.ds(pl.multiple_of(yy * 2 * MSG, 2 * MSG), 2 * MSG)
            send[st % NC, rows, :] = dot(pk[rows, :], xall[st, pl.ds(0, ALL), :]).astype(BF16)
            for cc in range(2):
                e = yy * 2 + cc

                @pl.when(e != ep)
                def _():
                    d_copy(st, (e - ep + PEERS) % PEERS).start()

            return 0

        lax.fori_loop(0, 4, body, 0)
        own_copy(st).start()

    def u_body(c, _):
        @pl.when(c + 2 < 2 * NC)
        def _():
            forward(c + 2)

        pack(c)
        part = dot(rwt[c], xall[c, pl.ds(0, ALL), :], NT)

        @pl.when(c == 0)
        def _():
            zt[...] = part

        @pl.when(c > 0)
        def _():
            zt[...] += part

        return 0

    lax.fori_loop(0, NC, u_body, 0)

    for b in range(8):
        lanes = slice(b * 128, (b + 1) * 128)
        r = rts[b]
        ids = lax.broadcasted_iota(jnp.int32, (EXPERTS, 128), 0)
        mask = jnp.zeros((EXPERTS, 128), F32)
        for k in range(6):
            mask = mask + jnp.where(r[k : k + 1, :] == ids, 1.0, 0.0)
        sg = jax.nn.sigmoid(zt[:, lanes])
        zt[:, lanes] = sg
        rowg[:, lanes] = jnp.sum(mask * sg, axis=0, keepdims=True)
    gt = (zt[pl.ds(pl.multiple_of(ts * PEERS, PEERS), PEERS), :] / rowg[...]).astype(BF16)

    def g_copy(i):
        e = (ep + i) % PEERS
        return remote(gs.at[e], gr.at[ep], g_ss.at[i - 1], g_rs.at[i - 1], at_ep(e))

    for d in range(PEERS):
        gs[d, :, 0:MSG] = dot(gt, pk[d * MSG : (d + 1) * MSG, :], NT)[d : d + 1, :] + jnp.zeros((8, MSG), F32)
        gs[d, :, MSG:256] = jnp.zeros((8, 256 - MSG), F32)
    gr[ep] = gs[ep]
    for i in range(1, PEERS):
        g_copy(i).start()

    def wait_d(st):
        for i in range(1, PEERS):
            d_copy(st, i).wait_recv()
        own_copy(st).wait()

    NTILE = ROWS // 3

    def ab_body(c, _):
        for i in range(1, PEERS):
            d_copy(c, i).wait_send()

        @pl.when(c + 2 < NC)
        def _():
            forward(NC + c + 2)

        wait_d(c)
        for i in (1, 3, 2):
            a_copy(c, i).wait_send()
            b_copy(c, i).wait_send()
        pack(NC + c)
        for i in range(2):
            wcopy_dyn(i, c).wait()

        def tile(t, _):
            cols = pl.ds(pl.multiple_of(t * NTILE, NTILE), NTILE)
            rows = rall[c, cols, :]
            pa = dot(wg[c], rows, NT)
            pb = dot(wu[c], rows, NT)

            @pl.when(c == 0)
            def _():
                acc1[:, cols] = pa
                acc2[:, cols] = pb

            @pl.when(c > 0)
            def _():
                acc1[:, cols] += pa
                acc2[:, cols] += pb

            return 0

        lax.fori_loop(0, 3, tile, 0)
        return 0

    def wcopy_dyn(i, c):
        src, dst = ((wg_in, wg), (wu_in, wu), (wd_in, wd))[i]
        return pltpu.make_async_copy(
            src.at[:, pl.ds(pl.multiple_of(c * CW, CW), CW)], dst.at[c], wsem.at[i, c]
        )

    lax.fori_loop(0, NC, ab_body, 0)

    def drain(st, _):
        for i in (1, 3, 2):
            a_copy(st, i).wait_send()
            b_copy(st, i).wait_send()
        return 0

    lax.fori_loop(NC, 2 * NC, drain, 0)
    for i in range(1, 4):
        pl.semaphore_signal(free_sem, inc=1, device_id=at_xz((z + i) % 4, x), device_id_type=MESH)
        pl.semaphore_signal(free_sem, inc=1, device_id=at_xz(z, (x + i) % 4), device_id_type=MESH)

    FT = 32

    def act_body(t, _):
        f = pl.ds(pl.multiple_of(t * FT, FT), FT)
        a, b = acc1[f, :], acc2[f, :]
        sg = jax.nn.sigmoid(a)
        act = a * sg
        h[f, :] = (act * b).astype(BF16)
        s[f, :] = act.astype(BF16)
        q[f, :] = (b * sg * (1.0 + a * (1.0 - sg))).astype(BF16)
        return 0

    lax.fori_loop(0, SH // FT, act_body, 0)

    for i in range(1, PEERS):
        g_copy(i).wait_recv()
    total = jnp.zeros((8, ROWS + 128), F32)
    zpad = jnp.zeros((8, ROWS + 128 - 256), F32)
    for e in range(PEERS):
        piece = jnp.concatenate([gr[e], zpad], axis=1)
        total = total + (pltpu.roll(piece, e * MSG, 1) if e else piece)
    gwrow[...] = total[:, 0:ROWS]

    def p_body(c, _):
        wait_d(NC + c)
        wcopy_dyn(2, c).wait()

        def tile(t, _):
            cols = pl.ds(pl.multiple_of(t * NTILE, NTILE), NTILE)
            pp = dot(wd[c], rall[NC + c, cols, :], NT)

            @pl.when(c == 0)
            def _():
                acc1[:, cols] = pp

            @pl.when(c > 0)
            def _():
                acc1[:, cols] += pp

            return 0

        lax.fori_loop(0, 3, tile, 0)
        return 0

    lax.fori_loop(0, NC, p_body, 0)

    dgrow[...] = jnp.zeros_like(dgrow)
    GT = 128

    def grad_body(t, _):
        f = pl.ds(pl.multiple_of(t * GT, GT), GT)
        part = jnp.zeros((8, ROWS), F32)
        gw = gwrow[0:1, :]
        for k in range(GT // 16):
            fk = pl.ds(pl.multiple_of(t * GT + k * 16, 16), 16)
            p = acc1[fk, :]
            hh = h[fk, :].astype(F32)
            prod = hh * p
            part = part + prod[0:8] + prod[8:16]
            dh = p * gw
            q[fk, :] = (dh * q[fk, :].astype(F32)).astype(BF16)
            s[fk, :] = (dh * s[fk, :].astype(F32)).astype(BF16)
            h[fk, :] = (hh * gw).astype(BF16)
        dgrow[...] += part
        da[:, f] = jnp.transpose(q[f, :])
        db[:, f] = jnp.transpose(s[f, :])
        return 0

    lax.fori_loop(0, SH // GT, grad_body, 0)

    def dg_copy(i):
        e = (ep + i) % PEERS
        return remote(ds_.at[e], dr.at[ep], dg_ss.at[i - 1], dg_rs.at[i - 1], at_ep(e))

    dg = jnp.sum(dgrow[...], axis=0, keepdims=True) + jnp.zeros((8, ROWS), F32)
    dg = jnp.concatenate([dg, jnp.zeros((8, 128), F32)], axis=1)
    keep = lax.broadcasted_iota(jnp.int32, (8, 256), 1) < MSG
    for e in range(PEERS):
        moved = pltpu.roll(dg, ROWS + 128 - e * MSG, 1) if e else dg
        ds_[e] = jnp.where(keep, moved[:, 0:256], 0.0)
    dr[ep] = ds_[ep]
    for i in range(1, PEERS):
        dg_copy(i).start()

    def ret_copy(c, i):
        e = (ep + i) % PEERS
        return remote(
            send.at[c, pl.ds(pl.multiple_of(e * MSG, MSG), MSG)],
            xall.at[c, own_rows],
            r_ss.at[c, i - 1],
            r_rs.at[c, i - 1],
            at_ep(e),
        )

    def own_ret(c):
        return pltpu.make_async_copy(send.at[c, own_rows], xall.at[c, own_rows], lsem.at[c])

    def ret_body(c, _):
        for i in range(1, PEERS):
            d_copy(NC + c, i).wait_send()

        def body(i, _):
            yy = (y + 1 + i) % 4
            rows = pl.ds(pl.multiple_of(yy * 2 * MSG, 2 * MSG), 2 * MSG)
            send[c, rows, :] = (dot(da[rows, :], wg[c]) + dot(db[rows, :], wu[c])).astype(BF16)
            for cc in range(2):
                e = yy * 2 + cc

                @pl.when(e != ep)
                def _():
                    ret_copy(c, (e - ep + PEERS) % PEERS).start()

            return 0

        lax.fori_loop(0, 4, body, 0)
        own_ret(c).start()
        return 0

    lax.fori_loop(0, NC, ret_body, 0)

    for b in range(8):
        lanes = slice(b * 128, (b + 1) * 128)
        da[lanes, 0:KA] = jnp.transpose(pk[0:KA, lanes])
        db[lanes, 0:KB] = jnp.transpose(pk[KA:ROWS, lanes])

    def out_copy(i, c):
        src, dst = ((wg, gg_out), (wu, gu_out), (wd, gd_out))[i]
        return pltpu.make_async_copy(
            src.at[c], dst.at[:, pl.ds(pl.multiple_of(c * CW, CW), CW)], osem.at[i, c]
        )

    MT = 256

    def wgrad_body(c, _):
        gaccum[c] = jnp.zeros((8, CW), F32)

        def tile(t, _):
            f = pl.ds(pl.multiple_of(t * MT, MT), MT)
            ga = dot(q[f, :], rall[c])
            part = jnp.sum(ga * wg[c, f, :].astype(F32), axis=0, keepdims=True)
            wg[c, f, :] = ga.astype(BF16)
            gb = dot(s[f, :], rall[c])
            part = part + jnp.sum(gb * wu[c, f, :].astype(F32), axis=0, keepdims=True)
            wu[c, f, :] = gb.astype(BF16)
            gaccum[c] += part + jnp.zeros((8, CW), F32)
            wd[c, f, :] = dot(h[f, :], rall[NC + c]).astype(BF16)
            return 0

        lax.fori_loop(0, SH // MT, tile, 0)
        for i in range(3):
            out_copy(i, c).start()
        return 0

    lax.fori_loop(0, NC, wgrad_body, 0)
    for c in range(NC):
        gn_out[:, c * CW : (c + 1) * CW] = gaccum[c]

    def dt_copy(i):
        p = (me + i) % SRC
        zz, xx = p // 4, p % 4
        return remote(dgt.at[zz * 2 + xx // 2], dgr.at[me], dt_ss.at[i - 1], dt_rs.at[i - 1], at_xz(zz, xx))

    for i in range(1, PEERS):
        dg_copy(i).wait_recv()
    for d in range(PEERS):
        hi, lo = split(dr[d][:, 0:MSG])
        rows = pk[d * MSG : (d + 1) * MSG, :]
        got = dot(hi, rows) + dot(lo, rows)
        for b in range(8):
            dgt[b, d : d + 1, :] = got[0:1, b * 128 : (b + 1) * 128]
    dgr[me] = dgt[myb]
    for i in range(1, SRC):
        dt_copy(i).start()

    pl.semaphore_wait(free_sem, 6)

    def z_copy(c, i):
        zz = (z + i) % 4
        return remote(
            send.at[c, pl.ds(pl.multiple_of(zz * 4 * TOK, 4 * TOK), 4 * TOK)],
            xall.at[NC + c, pl.ds((i - 1) * 4 * TOK, 4 * TOK)],
            z_ss.at[c, i - 1],
            z_rs.at[c, i - 1],
            at_xz(zz, x),
        )

    def x_copy(c, i):
        xx = (x + i) % 4
        return remote(
            send.at[c, pl.ds(pl.multiple_of(line + xx * TOK, TOK), TOK)],
            xall.at[NC + c, pl.ds(12 * TOK + (i - 1) * TOK, TOK)],
            x_ss.at[c, i - 1],
            x_rs.at[c, i - 1],
            at_xz(z, xx),
        )

    def comb_body(c, _):
        for i in range(1, PEERS):
            ret_copy(c, i).wait_recv()
            ret_copy(c, i).wait_send()
        own_ret(c).wait()

        def body(i, _):
            zz = (z + 1 + i) % 4
            rows = pl.ds(pl.multiple_of(zz * 4 * TOK, 4 * TOK), 4 * TOK)
            low = dot(da[rows, 0:KA], xall[c, 0:KA, :])
            send[c, rows, :] = (low + dot(db[rows, 0:KB], xall[c, KA:ROWS, :])).astype(BF16)

            @pl.when(i < 3)
            def _():
                z_copy(c, i + 1).start()

            return 0

        lax.fori_loop(0, 4, body, 0)
        return 0

    def z_sum(c):
        for i in (1, 3, 2):
            z_copy(c, i).wait_recv()
        rows = pl.ds(line, 4 * TOK)
        tot = send[c, rows, :].astype(F32)
        for i in range(3):
            tot = tot + xall[NC + c, i * 4 * TOK : (i + 1) * 4 * TOK, :].astype(F32)
        send[c, rows, :] = tot.astype(BF16)
        for i in (1, 3, 2):
            x_copy(c, i).start()

    def comb_loop(c, _):
        comb_body(c, 0)

        @pl.when(c > 0)
        def _():
            z_sum(c - 1)

        return 0

    lax.fori_loop(0, NC, comb_loop, 0)
    z_sum(NC - 1)

    for i in range(1, SRC):
        dt_copy(i).wait_recv()
    for t in range(8):
        zz, hh = t % 4, t // 4
        j = zz * 4 + hh * 2
        dzs[t * 8 : (t + 1) * 8, :] = dgr[j] + dgr[j + 1]
    lanes = pl.ds(pl.multiple_of(myb * 128, 128), 128)
    r = rt[...]
    ids = lax.broadcasted_iota(jnp.int32, (EXPERTS, 128), 0)
    mask = jnp.zeros((EXPERTS, 128), F32)
    for k in range(6):
        mask = mask + jnp.where(r[k : k + 1, :] == ids, 1.0, 0.0)
    sg = zt[:, lanes]
    tot = rowg[0:1, lanes]
    dg = dzs[...]
    mixed = jnp.sum(mask * (sg / tot) * dg, axis=0, keepdims=True)
    dz = mask * ((dg - mixed) / tot) * sg * (1.0 - sg)
    pad = jnp.concatenate([dz, jnp.zeros((64, 128), F32)], axis=0)
    dzs2 = jnp.transpose(pad)
    acc1[0:128, 0:128] = dzs2
    dz_own = acc1[pl.ds(pl.multiple_of(dp * TOK, TOK), TOK), 0:EXPERTS]
    hi, lo = split(dz_own)
    wide = tok[...].astype(F32)
    inv = lax.rsqrt(jnp.mean(wide * wide, axis=1, keepdims=True) + 1e-06)
    u_own = (wide * inv * gain[...]).astype(BF16)
    gr_out[...] = dot(hi, u_own, TN) + dot(lo, u_own, TN)

    for c in range(NC):
        cols = slice(c * CW, (c + 1) * CW)
        du = dot(hi, rwt[c]) + dot(lo, rwt[c])
        for i in (1, 3, 2):
            x_copy(c, i).wait_recv()
        du = du + send[c, pl.ds(mine, TOK), :].astype(F32)
        for i in range(3):
            du = du + xall[NC + c, (12 + i) * TOK : (13 + i) * TOK, :].astype(F32)
        gx_out[:, cols] = du * gain[:, cols]
    v = wide * inv
    scaled = gx_out[...]
    gx_out[...] = inv * scaled - v * inv * jnp.mean(v * scaled, axis=1, keepdims=True)

    def drain2(c, _):
        for i in (1, 3, 2):
            z_copy(c, i).wait_send()
            x_copy(c, i).wait_send()
        for i in range(3):
            out_copy(i, c).wait()
        return 0

    lax.fori_loop(0, NC, drain2, 0)
    for i in range(1, PEERS):
        rt_copy(i).wait_send()
        g_copy(i).wait_send()
        dg_copy(i).wait_send()
    for i in range(1, SRC):
        dt_copy(i).wait_send()


def call(tok, dy, rt, gain, rwt, wg, wu, wd):
    vmem = pl.BlockSpec(memory_space=pltpu.VMEM)
    hbm = pl.BlockSpec(memory_space=pl.ANY)
    V = pltpu.VMEM
    S = pltpu.SemaphoreType.DMA
    weight = jax.ShapeDtypeStruct((SH, D), BF16)
    return pl.pallas_call(
        kernel,
        out_shape=(
            jax.ShapeDtypeStruct((TOK, D), F32),
            jax.ShapeDtypeStruct((EXPERTS, D), F32),
            jax.ShapeDtypeStruct((8, D), F32),
            weight, weight, weight,
        ),
        in_specs=[vmem] * 5 + [hbm] * 3,
        out_specs=(vmem, vmem, vmem, hbm, hbm, hbm),
        scratch_shapes=[
            V((2 * NC, ROWS, CW), BF16),
            V((2 * NC, ROWS, CW), BF16),
            V((NC, ROWS, CW), BF16),
            V((NC, SH, CW), BF16), V((NC, SH, CW), BF16), V((NC, SH, CW), BF16),
            V((SH, ROWS), F32), V((SH, ROWS), F32),
            V((SH, ROWS), BF16), V((SH, ROWS), BF16), V((SH, ROWS), BF16),
            V((ROWS, SH), BF16), V((ROWS, SH), BF16),
            V((ROWS, ALL), BF16),
            V((8, 8, 128), jnp.int32),
            V((EXPERTS, ALL), F32),
            V((16, ALL), jnp.int32),
            V((8, 8, 256), F32), V((8, 8, 256), F32),
            V((8, 8, 256), F32), V((8, 8, 256), F32),
            V((8, 8, 128), F32), V((SRC, 8, 128), F32),
            V((8, ROWS), F32), V((8, ROWS), F32),
            V((1, ALL), F32), V((EXPERTS, 128), F32),
            V((NC, 8, CW), F32),
            S((3, NC)), S((3, NC)), S((2 * NC,)),
            S((7,)), S((7,)),
            S((2 * NC, 3)), S((2 * NC, 3)), S((2 * NC, 3)), S((2 * NC, 3)),
            S((2 * NC, 7)), S((2 * NC, 7)),
            S((7,)), S((7,)), S((7,)), S((7,)),
            S((15,)), S((15,)),
            S((NC, 7)), S((NC, 7)),
            S((NC, 3)), S((NC, 3)), S((NC, 3)), S((NC, 3)),
            pltpu.SemaphoreType.REGULAR,
        ],
        compiler_params=pltpu.CompilerParams(
            collective_id=0, has_side_effects=True, vmem_limit_bytes=VMEM_LIMIT
        ),
    )(tok, dy, rt, gain, rwt, wg, wu, wd)


VMEM_LIMIT = 65472 * 1024


def local(tokens, out_grad, routes, norm_gain, router_w, w_gate, w_up, w_down):
    rt = jnp.pad(routes[0].T, ((0, 2), (0, 0)), constant_values=-1)
    gain = norm_gain.astype(F32)[None]
    rwt = router_w.T.reshape(EXPERTS, NC, CW).transpose(1, 0, 2)
    gx, grt, gn, gg, gu, gd = call(
        tokens[0], out_grad[0], rt, gain, rwt, w_gate[0], w_up[0], w_down[0]
    )
    both = jnp.concatenate([grt, gn[0:1]], axis=0)
    both = lax.psum(both, ("ts", "dp", "ep"))
    grt = both[0:EXPERTS]
    wide_rw = router_w.astype(F32)
    grad_router = grt.T
    grad_gain = (both[EXPERTS] + jnp.sum(wide_rw * grad_router, axis=1)) / gain[0]
    return (gx[None], gg[None], gu[None], gd[None], grad_router, grad_gain)


def solution(mesh):
    split3 = P(("ts", "ep"), "dp", None)
    return jax.shard_map(
        local,
        mesh=mesh,
        in_specs=(split3, split3, P(("ts", "ep"), None, None), P(), P(), split3, split3, split3),
        out_specs=(split3, split3, split3, split3, P(), P()),
        check_vma=False,
    )
```

```python
import jax
import jax.numpy as jnp
from jax import lax
from jax.experimental import pallas as pl
from jax.experimental.pallas import tpu as pltpu
from jax.sharding import PartitionSpec as P

MESH = pl.DeviceIdType.MESH
F32 = jnp.float32
BF16 = jnp.bfloat16
D = 2560
NC = 4
CW = D // NC
TOK = 64
MOST = 9
SRC = 16
MSG = SRC * MOST
PEERS = 8
ROWS = PEERS * MSG
ALL = SRC * TOK
SH = 768
EXPERTS = 64
KA = 640
KB = ROWS - KA
NT = (((1,), (1,)), ((), ()))
TN = (((0,), (0,)), ((), ()))


def dot(a, b, dims=(((1,), (0,)), ((), ()))):
    return lax.dot_general(a, b, dims, preferred_element_type=F32)


def split(a):
    hi = a.astype(BF16)
    return hi, (a - hi.astype(F32)).astype(BF16)


def kernel(
    tok, dy, rt, gain, rwt, wg_in, wu_in, wd_in,
    gx_out, gr_out, gn_out, gg_out, gu_out, gd_out,
    xall, rall, send, wg, wu, wd, acc1, acc2, q, s, h, da, db, pk,
    rts, zt, slots, gs, gr, ds_, dr, dgt, dgr, gwrow, dgrow, rowg, dzs, gaccum, zr, row_s, grt,
    wsem, osem, lsem,
    rt_ss, rt_rs, a_ss, a_rs, b_ss, b_rs, d_ss, d_rs, g_ss, g_rs, dg_ss, dg_rs, dt_ss, dt_rs,
    r_ss, r_rs, z_ss, z_rs, x_ss, x_rs, zb_ss, zb_rs, zs_ss, zs_rs, p1_ss, p1_rs, p2_ss, p2_rs, p3_ss, p3_rs, free_sem,
):
    ts, dp, ep = lax.axis_index("ts"), lax.axis_index("dp"), lax.axis_index("ep")
    xh, z = ts // 4, ts % 4
    x = xh * 2 + dp
    y, core = ep // 2, ep % 2
    me = z * 4 + x

    def at_xz(zz, xx):
        return ((xx // 2) * 4 + zz, xx % 2, ep)

    def at_ep(e):
        return (ts, dp, e)

    def remote(src, dst, ss, rs, dev):
        return pltpu.make_async_remote_copy(
            src_ref=src, dst_ref=dst, send_sem=ss, recv_sem=rs, device_id=dev, device_id_type=MESH
        )

    def wcopy(i, c):
        src, dst = ((wg_in, wg), (wu_in, wu), (wd_in, wd))[i]
        return pltpu.make_async_copy(src.at[:, pl.ds(c * CW, CW)], dst.at[c], wsem.at[i, c])

    for c in range(NC):
        for i in range(3):
            wcopy(i, c).start()

    barrier = pltpu.get_barrier_semaphore()
    for i in range(1, PEERS):
        pl.semaphore_signal(barrier, inc=1, device_id=at_ep((ep + i) % PEERS), device_id_type=MESH)
    for i in range(1, SRC):
        p = (me + i) % SRC
        pl.semaphore_signal(barrier, inc=1, device_id=at_xz(p // 4, p % 4), device_id_type=MESH)
    pl.semaphore_wait(barrier, PEERS - 1 + SRC - 1)

    myb = z * 2 + xh
    rts[myb] = rt[...]

    def rt_copy(i):
        t = (ts + i) % 8
        return remote(rt, rts.at[myb], rt_ss.at[i - 1], rt_rs.at[i - 1], (t, dp, ep))

    for i in range(1, 8):
        rt_copy(i).start()

    mine = pl.multiple_of(me * TOK, TOK)
    wide = tok[...].astype(F32)
    inv = lax.rsqrt(jnp.mean(wide * wide, axis=1, keepdims=True) + 1e-06)
    u_own = (wide * inv * gain[...]).astype(BF16)
    for c in range(NC):
        xall[c, pl.ds(mine, TOK), :] = u_own[:, c * CW : (c + 1) * CW]
        xall[NC + c, pl.ds(mine, TOK), :] = dy[:, c * CW : (c + 1) * CW]

    def a_copy(st, i):
        block = xall.at[st, pl.ds(mine, TOK)]
        return remote(block, block, a_ss.at[st, i - 1], a_rs.at[st, i - 1], at_xz(z, (x + i) % 4))

    line = pl.multiple_of(z * 4 * TOK, 4 * TOK)

    def b_copy(st, i):
        block = xall.at[st, pl.ds(line, 4 * TOK)]
        return remote(block, block, b_ss.at[st, i - 1], b_rs.at[st, i - 1], at_xz((z + i) % 4, x))

    for st in range(2 * NC):
        for i in (1, 3, 2):
            a_copy(st, i).start()

    def forward(st):
        for i in (1, 3, 2):
            a_copy(st, i).wait_recv()
        for i in (1, 3, 2):
            b_copy(st, i).start()

    forward(0)
    forward(1)

    for i in range(1, 8):
        rt_copy(i).wait_recv()
    lane = lax.broadcasted_iota(jnp.int32, (128, 128), 1)
    sub = lax.broadcasted_iota(jnp.int32, (128, 128), 0)
    before = jnp.where((sub < lane) & ((sub // TOK) == (lane // TOK)), 1.0, 0.0).astype(BF16)
    for b in range(8):
        r = rts[b]
        ids = lax.broadcasted_iota(jnp.int32, (16, 128), 0)
        own = jnp.zeros((16, 128), F32)
        for k in range(6):
            own = own + jnp.where((r[k : k + 1, :] == ts * PEERS + ids) & (ids < PEERS), 1.0, 0.0)
        rank = dot(own.astype(BF16), before)
        half = lax.broadcasted_iota(jnp.int32, (16, 128), 1) // TOK
        slot = jnp.where(own > 0.5, (2 * b + half) * MOST + rank.astype(jnp.int32), -1)
        slots[:, b * 128 : (b + 1) * 128] = slot

    def slot_body(d, _):
        row = slots[pl.ds(d, 1), :]
        hit = lax.broadcasted_iota(jnp.int32, (MSG, ALL), 0) == row
        pk[pl.ds(pl.multiple_of(d * MSG, MSG), MSG), :] = jnp.where(hit, 1.0, 0.0).astype(BF16)
        return 0

    lax.fori_loop(0, PEERS, slot_body, 0)
    def d_copy(st, i):
        e = (ep + i) % PEERS
        return remote(
            send.at[st % NC, pl.ds(pl.multiple_of(e * MSG, MSG), MSG)],
            rall.at[st, pl.ds(pl.multiple_of(ep * MSG, MSG), MSG)],
            d_ss.at[st, i - 1],
            d_rs.at[st, i - 1],
            at_ep(e),
        )

    own_rows = pl.ds(pl.multiple_of(ep * MSG, MSG), MSG)

    def own_copy(st):
        return pltpu.make_async_copy(send.at[st % NC, own_rows], rall.at[st, own_rows], lsem.at[st])

    def pack(st):
        for i in (1, 3, 2):
            b_copy(st, i).wait_recv()

        def body(i, _):
            yy = (y + 1 + i) % 4
            rows = pl.ds(pl.multiple_of(yy * 2 * MSG, 2 * MSG), 2 * MSG)
            send[st % NC, rows, :] = dot(pk[rows, :], xall[st, pl.ds(0, ALL), :]).astype(BF16)
            for cc in range(2):
                e = yy * 2 + cc

                @pl.when(e != ep)
                def _():
                    d_copy(st, (e - ep + PEERS) % PEERS).start()

            return 0

        lax.fori_loop(0, 4, body, 0)
        own_copy(st).start()

    def u_body(c, _):
        @pl.when(c + 2 < 2 * NC)
        def _():
            forward(c + 2)

        pack(c)
        part = dot(rwt[c], xall[c, pl.ds(0, ALL), :], NT)

        @pl.when(c == 0)
        def _():
            zt[...] = part

        @pl.when(c > 0)
        def _():
            zt[...] += part

        return 0

    lax.fori_loop(0, NC, u_body, 0)

    for b in range(8):
        lanes = slice(b * 128, (b + 1) * 128)
        r = rts[b]
        ids = lax.broadcasted_iota(jnp.int32, (EXPERTS, 128), 0)
        mask = jnp.zeros((EXPERTS, 128), F32)
        for k in range(6):
            mask = mask + jnp.where(r[k : k + 1, :] == ids, 1.0, 0.0)
        sg = jax.nn.sigmoid(zt[:, lanes])
        zt[:, lanes] = sg
        rowg[:, lanes] = jnp.sum(mask * sg, axis=0, keepdims=True)
    gt = (zt[pl.ds(pl.multiple_of(ts * PEERS, PEERS), PEERS), :] / rowg[...]).astype(BF16)

    def g_copy(i):
        e = (ep + i) % PEERS
        return remote(gs.at[e], gr.at[ep], g_ss.at[i - 1], g_rs.at[i - 1], at_ep(e))

    for d in range(PEERS):
        gs[d, :, 0:MSG] = dot(gt, pk[d * MSG : (d + 1) * MSG, :], NT)[d : d + 1, :] + jnp.zeros((8, MSG), F32)
        gs[d, :, MSG:256] = jnp.zeros((8, 256 - MSG), F32)
    gr[ep] = gs[ep]
    for i in range(1, PEERS):
        g_copy(i).start()

    def wait_d(st):
        for i in range(1, PEERS):
            d_copy(st, i).wait_recv()
        own_copy(st).wait()

    NTILE = ROWS // 3

    def ab_body(c, _):
        for i in range(1, PEERS):
            d_copy(c, i).wait_send()

        @pl.when(c + 2 < NC)
        def _():
            forward(NC + c + 2)

        wait_d(c)
        for i in (1, 3, 2):
            a_copy(c, i).wait_send()
            b_copy(c, i).wait_send()
        pack(NC + c)
        for i in range(2):
            wcopy_dyn(i, c).wait()

        def tile(t, _):
            cols = pl.ds(pl.multiple_of(t * NTILE, NTILE), NTILE)
            rows = rall[c, cols, :]
            pa = dot(wg[c], rows, NT)
            pb = dot(wu[c], rows, NT)

            @pl.when(c == 0)
            def _():
                acc1[:, cols] = pa
                acc2[:, cols] = pb

            @pl.when(c > 0)
            def _():
                acc1[:, cols] += pa
                acc2[:, cols] += pb

            return 0

        lax.fori_loop(0, 3, tile, 0)
        return 0

    def wcopy_dyn(i, c):
        src, dst = ((wg_in, wg), (wu_in, wu), (wd_in, wd))[i]
        return pltpu.make_async_copy(
            src.at[:, pl.ds(pl.multiple_of(c * CW, CW), CW)], dst.at[c], wsem.at[i, c]
        )

    lax.fori_loop(0, NC, ab_body, 0)

    def drain(st, _):
        for i in (1, 3, 2):
            a_copy(st, i).wait_send()
            b_copy(st, i).wait_send()
        return 0

    lax.fori_loop(NC, 2 * NC, drain, 0)
    for i in range(1, 4):
        pl.semaphore_signal(free_sem.at[0], inc=1, device_id=at_xz((z + i) % 4, x), device_id_type=MESH)
        pl.semaphore_signal(free_sem.at[0], inc=1, device_id=at_xz(z, (x + i) % 4), device_id_type=MESH)

    FT = 32

    def act_body(t, _):
        f = pl.ds(pl.multiple_of(t * FT, FT), FT)
        a, b = acc1[f, :], acc2[f, :]
        sg = jax.nn.sigmoid(a)
        act = a * sg
        h[f, :] = (act * b).astype(BF16)
        s[f, :] = act.astype(BF16)
        q[f, :] = (b * sg * (1.0 + a * (1.0 - sg))).astype(BF16)
        return 0

    lax.fori_loop(0, SH // FT, act_body, 0)

    for i in range(1, PEERS):
        g_copy(i).wait_recv()
    total = jnp.zeros((8, ROWS + 128), F32)
    zpad = jnp.zeros((8, ROWS + 128 - 256), F32)
    for e in range(PEERS):
        piece = jnp.concatenate([gr[e], zpad], axis=1)
        total = total + (pltpu.roll(piece, e * MSG, 1) if e else piece)
    gwrow[...] = total[:, 0:ROWS]

    def p_body(c, _):
        wait_d(NC + c)
        wcopy_dyn(2, c).wait()

        def tile(t, _):
            cols = pl.ds(pl.multiple_of(t * NTILE, NTILE), NTILE)
            pp = dot(wd[c], rall[NC + c, cols, :], NT)

            @pl.when(c == 0)
            def _():
                acc1[:, cols] = pp

            @pl.when(c > 0)
            def _():
                acc1[:, cols] += pp

            return 0

        lax.fori_loop(0, 3, tile, 0)
        return 0

    lax.fori_loop(0, NC, p_body, 0)

    dgrow[...] = jnp.zeros_like(dgrow)
    GT = 128

    def grad_body(t, _):
        f = pl.ds(pl.multiple_of(t * GT, GT), GT)
        part = jnp.zeros((8, ROWS), F32)
        gw = gwrow[0:1, :]
        for k in range(GT // 16):
            fk = pl.ds(pl.multiple_of(t * GT + k * 16, 16), 16)
            p = acc1[fk, :]
            hh = h[fk, :].astype(F32)
            prod = hh * p
            part = part + prod[0:8] + prod[8:16]
            dh = p * gw
            q[fk, :] = (dh * q[fk, :].astype(F32)).astype(BF16)
            s[fk, :] = (dh * s[fk, :].astype(F32)).astype(BF16)
            h[fk, :] = (hh * gw).astype(BF16)
        dgrow[...] += part
        da[:, f] = jnp.transpose(q[f, :])
        db[:, f] = jnp.transpose(s[f, :])
        return 0

    lax.fori_loop(0, SH // GT, grad_body, 0)

    def dg_copy(i):
        e = (ep + i) % PEERS
        return remote(ds_.at[e], dr.at[ep], dg_ss.at[i - 1], dg_rs.at[i - 1], at_ep(e))

    dg = jnp.sum(dgrow[...], axis=0, keepdims=True) + jnp.zeros((8, ROWS), F32)
    dg = jnp.concatenate([dg, jnp.zeros((8, 128), F32)], axis=1)
    keep = lax.broadcasted_iota(jnp.int32, (8, 256), 1) < MSG
    for e in range(PEERS):
        moved = pltpu.roll(dg, ROWS + 128 - e * MSG, 1) if e else dg
        ds_[e] = jnp.where(keep, moved[:, 0:256], 0.0)
    dr[ep] = ds_[ep]
    for i in range(1, PEERS):
        dg_copy(i).start()

    def ret_copy(c, i):
        e = (ep + i) % PEERS
        return remote(
            send.at[c, pl.ds(pl.multiple_of(e * MSG, MSG), MSG)],
            xall.at[c, own_rows],
            r_ss.at[c, i - 1],
            r_rs.at[c, i - 1],
            at_ep(e),
        )

    def own_ret(c):
        return pltpu.make_async_copy(send.at[c, own_rows], xall.at[c, own_rows], lsem.at[c])

    def ret_body(c, _):
        for i in range(1, PEERS):
            d_copy(NC + c, i).wait_send()

        def body(i, _):
            yy = (y + 1 + i) % 4
            rows = pl.ds(pl.multiple_of(yy * 2 * MSG, 2 * MSG), 2 * MSG)
            send[c, rows, :] = (dot(da[rows, :], wg[c]) + dot(db[rows, :], wu[c])).astype(BF16)
            for cc in range(2):
                e = yy * 2 + cc

                @pl.when(e != ep)
                def _():
                    ret_copy(c, (e - ep + PEERS) % PEERS).start()

            return 0

        lax.fori_loop(0, 4, body, 0)
        own_ret(c).start()
        return 0

    lax.fori_loop(0, NC, ret_body, 0)

    for b in range(8):
        lanes = slice(b * 128, (b + 1) * 128)
        da[lanes, 0:KA] = jnp.transpose(pk[0:KA, lanes])
        db[lanes, 0:KB] = jnp.transpose(pk[KA:ROWS, lanes])

    def out_copy(i, c):
        src, dst = ((wg, gg_out), (wu, gu_out), (wd, gd_out))[i]
        return pltpu.make_async_copy(
            src.at[c], dst.at[:, pl.ds(pl.multiple_of(c * CW, CW), CW)], osem.at[i, c]
        )

    MT = 256

    def wgrad_body(c, _):
        gaccum[c] = jnp.zeros((8, CW), F32)

        def tile(t, _):
            f = pl.ds(pl.multiple_of(t * MT, MT), MT)
            ga = dot(q[f, :], rall[c])
            part = jnp.sum(ga * wg[c, f, :].astype(F32), axis=0, keepdims=True)
            wg[c, f, :] = ga.astype(BF16)
            gb = dot(s[f, :], rall[c])
            part = part + jnp.sum(gb * wu[c, f, :].astype(F32), axis=0, keepdims=True)
            wu[c, f, :] = gb.astype(BF16)
            gaccum[c] += part + jnp.zeros((8, CW), F32)
            wd[c, f, :] = dot(h[f, :], rall[NC + c]).astype(BF16)
            return 0

        lax.fori_loop(0, SH // MT, tile, 0)
        for i in range(3):
            out_copy(i, c).start()
        return 0

    def dt_copy(i):
        p = (me + i) % SRC
        zz, xx = p // 4, p % 4
        return remote(dgt.at[zz * 2 + xx // 2], dgr.at[me], dt_ss.at[i - 1], dt_rs.at[i - 1], at_xz(zz, xx))

    for i in range(1, PEERS):
        dg_copy(i).wait_recv()
    for d in range(PEERS):
        hi, lo = split(dr[d][:, 0:MSG])
        rows = pk[d * MSG : (d + 1) * MSG, :]
        got = dot(hi, rows) + dot(lo, rows)
        for b in range(8):
            dgt[b, d : d + 1, :] = got[0:1, b * 128 : (b + 1) * 128]
    dgr[me] = dgt[myb]
    for i in range(1, SRC):
        dt_copy(i).start()

    lax.fori_loop(0, 2, wgrad_body, 0)

    for i in range(1, SRC):
        dt_copy(i).wait_recv()
    for t in range(8):
        zz, hh = t % 4, t // 4
        j = zz * 4 + hh * 2
        dzs[t * 8 : (t + 1) * 8, :] = dgr[j] + dgr[j + 1]
    lanes = pl.ds(pl.multiple_of(myb * 128, 128), 128)
    r = rt[...]
    ids = lax.broadcasted_iota(jnp.int32, (EXPERTS, 128), 0)
    mask = jnp.zeros((EXPERTS, 128), F32)
    for k in range(6):
        mask = mask + jnp.where(r[k : k + 1, :] == ids, 1.0, 0.0)
    sg = zt[:, lanes]
    tot = rowg[0:1, lanes]
    dg = dzs[...]
    mixed = jnp.sum(mask * (sg / tot) * dg, axis=0, keepdims=True)
    dzs[...] = mask * ((dg - mixed) / tot) * sg * (1.0 - sg)

    def zb_copy(i):
        t = (ts + i) % 8
        return remote(
            dzs.at[pl.ds(pl.multiple_of(t * 8, 8), 8)], dgt.at[myb], zb_ss.at[i - 1], zb_rs.at[i - 1], (t, dp, ep)
        )

    for i in range(1, SRC):
        dt_copy(i).wait_send()
    dgt[myb] = dzs[pl.ds(pl.multiple_of(ts * 8, 8), 8), :]
    for i in range(1, 8):
        pl.semaphore_signal(free_sem.at[1], inc=1, device_id=((ts + i) % 8, dp, ep), device_id_type=MESH)
    pl.semaphore_wait(free_sem.at[1], 7)
    for i in range(1, 8):
        zb_copy(i).start()

    lax.fori_loop(2, NC, wgrad_body, 0)

    def zs_copy(i):
        e = (ep + i) % PEERS
        return remote(gs.at[e], zr.at[ep], zs_ss.at[i - 1], zs_rs.at[i - 1], at_ep(e))

    for i in range(1, 8):
        zb_copy(i).wait_recv()
    for i in range(1, PEERS):
        g_copy(i).wait_send()
    for d in range(PEERS):
        got = jnp.zeros((8, MSG), F32)
        for b in range(8):
            hi, lo = split(dgt[b])
            rows = pk[d * MSG : (d + 1) * MSG, b * 128 : (b + 1) * 128]
            got = got + dot(hi, rows, NT) + dot(lo, rows, NT)
        gs[d, :, 0:MSG] = got[d : d + 1, :] + jnp.zeros((8, MSG), F32)
    zr[ep] = gs[ep]
    for i in range(1, PEERS):
        zs_copy(i).start()

    def p1_copy(i):
        e = (ep + i) % PEERS
        return remote(
            row_s,
            acc2.at[pl.ds(pl.multiple_of(ep * 48, 8), 48), pl.ds(0, 128)],
            p1_ss.at[i - 1],
            p1_rs.at[i - 1],
            at_ep(e),
        )

    def router_row():
        for i in range(1, PEERS):
            zs_copy(i).wait_recv()
        total = jnp.zeros((8, ROWS + 128), F32)
        zpad = jnp.zeros((8, ROWS + 128 - 256), F32)
        for e in range(PEERS):
            piece = jnp.concatenate([zr[e], zpad], axis=1)
            total = total + (pltpu.roll(piece, e * MSG, 1) if e else piece)
        hi, lo = split(total[:, 0:ROWS])
        for c in range(NC):
            row = (dot(hi, rall[c]) + dot(lo, rall[c]))[0:1, :]
            part = gaccum[c]
            for j in range(CW // 128):
                n = c * (CW // 128) + j
                row_s[n : n + 1, :] = row[:, j * 128 : (j + 1) * 128]
                row_s[24 + n : 25 + n, :] = part[0:1, j * 128 : (j + 1) * 128]
        for i in range(1, PEERS):
            p1_copy(i).start()
        acc2[pl.ds(pl.multiple_of(ep * 48, 8), 48), 0:128] = row_s[...]

    myrows = pl.ds(pl.multiple_of(ts * 8, 8), 8)

    def p2_copy(i):
        return remote(
            grt.at[myrows], grt.at[myrows], p2_ss.at[i - 1], p2_rs.at[i - 1], ((ts + i) % 8, dp, ep)
        )

    mygain = pl.ds(pl.multiple_of(me * 24, 8), 24)

    def p3_copy(i):
        p = (me + i) % SRC
        block = acc2.at[mygain, pl.ds(128, 128)]
        return remote(block, block, p3_ss.at[i - 1], p3_rs.at[i - 1], at_xz(p // 4, p % 4))

    def router_rows():
        for i in range(1, PEERS):
            p1_copy(i).wait_recv()
        for n in range(D // 128):
            rows = [acc2[e * 48 + n : e * 48 + n + 1, 0:128] for e in range(PEERS)]
            grt[myrows, n * 128 : (n + 1) * 128] = jnp.concatenate(rows, axis=0)
        tot = acc2[24:48, 0:128]
        for e in range(1, PEERS):
            tot = tot + acc2[e * 48 + 24 : (e + 1) * 48, 0:128]
        acc2[mygain, 128:256] = tot
        for i in range(1, 8):
            p2_copy(i).start()
        for i in range(1, SRC):
            p3_copy(i).start()

    pl.semaphore_wait(free_sem.at[0], 6)

    def z_copy(c, i):
        zz = (z + i) % 4
        return remote(
            send.at[c, pl.ds(pl.multiple_of(zz * 4 * TOK, 4 * TOK), 4 * TOK)],
            xall.at[NC + c, pl.ds((i - 1) * 4 * TOK, 4 * TOK)],
            z_ss.at[c, i - 1],
            z_rs.at[c, i - 1],
            at_xz(zz, x),
        )

    def x_copy(c, i):
        xx = (x + i) % 4
        return remote(
            send.at[c, pl.ds(pl.multiple_of(line + xx * TOK, TOK), TOK)],
            xall.at[NC + c, pl.ds(12 * TOK + (i - 1) * TOK, TOK)],
            x_ss.at[c, i - 1],
            x_rs.at[c, i - 1],
            at_xz(z, xx),
        )

    def comb_body(c, _):
        for i in range(1, PEERS):
            ret_copy(c, i).wait_recv()
            ret_copy(c, i).wait_send()
        own_ret(c).wait()

        def body(i, _):
            zz = (z + 1 + i) % 4
            rows = pl.ds(pl.multiple_of(zz * 4 * TOK, 4 * TOK), 4 * TOK)
            low = dot(da[rows, 0:KA], xall[c, 0:KA, :])
            send[c, rows, :] = (low + dot(db[rows, 0:KB], xall[c, KA:ROWS, :])).astype(BF16)

            @pl.when(i < 3)
            def _():
                z_copy(c, i + 1).start()

            return 0

        lax.fori_loop(0, 4, body, 0)
        return 0

    def z_sum(c):
        for i in (1, 3, 2):
            z_copy(c, i).wait_recv()
        rows = pl.ds(line, 4 * TOK)
        tot = send[c, rows, :].astype(F32)
        for i in range(3):
            tot = tot + xall[NC + c, i * 4 * TOK : (i + 1) * 4 * TOK, :].astype(F32)
        send[c, rows, :] = tot.astype(BF16)
        for i in (1, 3, 2):
            x_copy(c, i).start()

    def comb_loop(c, _):
        comb_body(c, 0)

        @pl.when(c > 0)
        def _():
            z_sum(c - 1)

        return 0

    comb_loop(0, 0)
    router_row()
    lax.fori_loop(1, NC - 1, comb_loop, 0)
    router_rows()
    comb_loop(NC - 1, 0)
    z_sum(NC - 1)

    pad = jnp.concatenate([dzs[...], jnp.zeros((64, 128), F32)], axis=0)
    acc1[0:128, 0:128] = jnp.transpose(pad)
    dz_own = acc1[pl.ds(pl.multiple_of(dp * TOK, TOK), TOK), 0:EXPERTS]
    hi, lo = split(dz_own)
    wide = tok[...].astype(F32)
    inv = lax.rsqrt(jnp.mean(wide * wide, axis=1, keepdims=True) + 1e-06)

    for i in range(1, 8):
        p2_copy(i).wait_recv()
    for i in range(1, SRC):
        p3_copy(i).wait_recv()
    tot = acc2[0:24, 128:256]
    for p in range(1, SRC):
        tot = tot + acc2[p * 24 : (p + 1) * 24, 128:256]
    for n in range(D // 128):
        cols = slice(n * 128, (n + 1) * 128)
        c, o = n * 128 // CW, n * 128 % CW
        g = grt[:, cols]
        gr_out[:, cols] = g
        along = jnp.sum(g * rwt[c, :, o : o + 128].astype(F32), axis=0, keepdims=True)
        gn_out[:, cols] = (along + tot[n : n + 1, :]) / gain[:, cols]

    for c in range(NC):
        cols = slice(c * CW, (c + 1) * CW)
        du = dot(hi, rwt[c]) + dot(lo, rwt[c])
        for i in (1, 3, 2):
            x_copy(c, i).wait_recv()
        du = du + send[c, pl.ds(mine, TOK), :].astype(F32)
        for i in range(3):
            du = du + xall[NC + c, (12 + i) * TOK : (13 + i) * TOK, :].astype(F32)
        gx_out[:, cols] = du * gain[:, cols]
    v = wide * inv
    scaled = gx_out[...]
    gx_out[...] = inv * scaled - v * inv * jnp.mean(v * scaled, axis=1, keepdims=True)

    def drain2(c, _):
        for i in (1, 3, 2):
            z_copy(c, i).wait_send()
            x_copy(c, i).wait_send()
        for i in range(3):
            out_copy(i, c).wait()
        return 0

    lax.fori_loop(0, NC, drain2, 0)
    for i in range(1, PEERS):
        rt_copy(i).wait_send()
        dg_copy(i).wait_send()
        zb_copy(i).wait_send()
        zs_copy(i).wait_send()
        p1_copy(i).wait_send()
        p2_copy(i).wait_send()
    for i in range(1, SRC):
        p3_copy(i).wait_send()


def call(tok, dy, rt, gain, rwt, wg, wu, wd):
    vmem = pl.BlockSpec(memory_space=pltpu.VMEM)
    hbm = pl.BlockSpec(memory_space=pl.ANY)
    V = pltpu.VMEM
    S = pltpu.SemaphoreType.DMA
    weight = jax.ShapeDtypeStruct((SH, D), BF16)
    return pl.pallas_call(
        kernel,
        out_shape=(
            jax.ShapeDtypeStruct((TOK, D), F32),
            jax.ShapeDtypeStruct((EXPERTS, D), F32),
            jax.ShapeDtypeStruct((1, D), F32),
            weight, weight, weight,
        ),
        in_specs=[vmem] * 5 + [hbm] * 3,
        out_specs=(vmem, vmem, vmem, hbm, hbm, hbm),
        scratch_shapes=[
            V((2 * NC, ROWS, CW), BF16),
            V((2 * NC, ROWS, CW), BF16),
            V((NC, ROWS, CW), BF16),
            V((NC, SH, CW), BF16), V((NC, SH, CW), BF16), V((NC, SH, CW), BF16),
            V((SH, ROWS), F32), V((SH, ROWS), F32),
            V((SH, ROWS), BF16), V((SH, ROWS), BF16), V((SH, ROWS), BF16),
            V((ROWS, SH), BF16), V((ROWS, SH), BF16),
            V((ROWS, ALL), BF16),
            V((8, 8, 128), jnp.int32),
            V((EXPERTS, ALL), F32),
            V((16, ALL), jnp.int32),
            V((8, 8, 256), F32), V((8, 8, 256), F32),
            V((8, 8, 256), F32), V((8, 8, 256), F32),
            V((8, 8, 128), F32), V((SRC, 8, 128), F32),
            V((8, ROWS), F32), V((8, ROWS), F32),
            V((1, ALL), F32), V((EXPERTS, 128), F32),
            V((NC, 8, CW), F32), V((8, 8, 256), F32), V((48, 128), F32), V((EXPERTS, D), F32),
            S((3, NC)), S((3, NC)), S((2 * NC,)),
            S((7,)), S((7,)),
            S((2 * NC, 3)), S((2 * NC, 3)), S((2 * NC, 3)), S((2 * NC, 3)),
            S((2 * NC, 7)), S((2 * NC, 7)),
            S((7,)), S((7,)), S((7,)), S((7,)),
            S((15,)), S((15,)),
            S((NC, 7)), S((NC, 7)),
            S((NC, 3)), S((NC, 3)), S((NC, 3)), S((NC, 3)),
            S((7,)), S((7,)), S((7,)), S((7,)), S((7,)), S((7,)),
            S((7,)), S((7,)), S((15,)), S((15,)),
            pltpu.SemaphoreType.REGULAR((2,)),
        ],
        compiler_params=pltpu.CompilerParams(
            collective_id=0, has_side_effects=True, vmem_limit_bytes=VMEM_LIMIT
        ),
    )(tok, dy, rt, gain, rwt, wg, wu, wd)


VMEM_LIMIT = 65472 * 1024


def local(tokens, out_grad, routes, norm_gain, router_w, w_gate, w_up, w_down):
    rt = jnp.pad(routes[0].T, ((0, 2), (0, 0)), constant_values=-1)
    gain = norm_gain.astype(F32)[None]
    rwt = router_w.T.reshape(EXPERTS, NC, CW).transpose(1, 0, 2)
    gx, grt, gn, gg, gu, gd = call(
        tokens[0], out_grad[0], rt, gain, rwt, w_gate[0], w_up[0], w_down[0]
    )
    return (gx[None], gg[None], gu[None], gd[None], grt.T, gn[0])


def solution(mesh):
    split3 = P(("ts", "ep"), "dp", None)
    return jax.shard_map(
        local,
        mesh=mesh,
        in_specs=(split3, split3, P(("ts", "ep"), None, None), P(), P(), split3, split3, split3),
        out_specs=(split3, split3, split3, split3, P(), P()),
        check_vma=False,
    )
```

```python
import jax
import jax.numpy as jnp
from jax import lax
from jax.experimental import pallas as pl
from jax.experimental.pallas import tpu as pltpu
from jax.sharding import PartitionSpec as P

MESH = pl.DeviceIdType.MESH
F32 = jnp.float32
BF16 = jnp.bfloat16
D = 2560
NC = 4
CW = D // NC
TOK = 64
MOST = 9
SRC = 16
MSG = SRC * MOST
PEERS = 8
ROWS = PEERS * MSG
ALL = SRC * TOK
SH = 768
EXPERTS = 64
KA = 640
KB = ROWS - KA
NT = (((1,), (1,)), ((), ()))
TN = (((0,), (0,)), ((), ()))


def dot(a, b, dims=(((1,), (0,)), ((), ()))):
    return lax.dot_general(a, b, dims, preferred_element_type=F32)


def split(a):
    hi = a.astype(BF16)
    return hi, (a - hi.astype(F32)).astype(BF16)


def split32(a):
    hi = a.astype(BF16)
    return hi, a - hi.astype(F32)


def kernel(
    tok, dy, rt, gain, rw_in, wg_in, wu_in, wd_in,
    gx_out, gr_out, gn_out, gg_out, gu_out, gd_out,
    xall, rall, send, wg, wu, wd, acc1, acc2, q, s, h, da, db, pk,
    rts, zt, slots, gs, gr, ds_, dr, dgt, dgr, gwrow, dgrow, rowg, dzs, gaccum, zr, row_s, rows8, cols8, rrow,
    wsem, osem, lsem,
    rt_ss, rt_rs, a_ss, a_rs, b_ss, b_rs, f_ss, f_rs, d_ss, d_rs, g_ss, g_rs, dg_ss, dg_rs, dt_ss, dt_rs,
    r_ss, r_rs, z_ss, z_rs, x_ss, x_rs, zb_ss, zb_rs, zs_ss, zs_rs, p1_ss, p1_rs, p2_ss, p2_rs, p3_ss, p3_rs, free_sem,
):
    ts, dp, ep = lax.axis_index("ts"), lax.axis_index("dp"), lax.axis_index("ep")
    xh, z = ts // 4, ts % 4
    x = xh * 2 + dp
    y, core = ep // 2, ep % 2
    g = z * (1 - core) + y * core
    b_at = y * (1 - core) + z * core
    me = g * 4 + x
    tsg = xh * 4 + g
    seat = core * 4 + b_at
    own_d = b_at * 2 + core

    def at_gx(gg, xx):
        zz = gg * (1 - core) + z * core
        yy = y * (1 - core) + gg * core
        return ((xx // 2) * 4 + zz, xx % 2, yy * 2 + core)

    def at_dest(d):
        bb = d // 2
        zz = z * (1 - core) + bb * core
        yy = bb * (1 - core) + y * core
        return (xh * 4 + zz, dp, yy * 2 + d % 2)

    def at_src(e):
        cs, bb = e // 4, e % 4
        zz = z * (1 - cs) + bb * cs
        yy = bb * (1 - cs) + y * cs
        return (xh * 4 + zz, dp, yy * 2 + cs)

    def d_at(e):
        cs = e // 4
        return (y * (1 - cs) + z * cs) * 2 + core

    def rows_of(k):
        return pl.ds(pl.multiple_of(k * MSG, MSG), MSG)

    def others(mine_, act):
        def body(k, _):
            @pl.when(k != mine_)
            def _():
                act(k)

            return 0

        lax.fori_loop(0, PEERS, body, 0)

    def remote(src, dst, ss, rs, dev):
        return pltpu.make_async_remote_copy(
            src_ref=src, dst_ref=dst, send_sem=ss, recv_sem=rs, device_id=dev, device_id_type=MESH
        )

    def wcopy(i, c):
        src, dst = ((wg_in, wg), (wu_in, wu), (wd_in, wd))[i]
        return pltpu.make_async_copy(src.at[:, pl.ds(c * CW, CW)], dst.at[c], wsem.at[i, c])

    for c in range(NC):
        for i in range(3):
            wcopy(i, c).start()

    barrier = pltpu.get_barrier_semaphore()
    def greet(zz, yy, xx, cc):
        pl.semaphore_signal(
            barrier, inc=1, device_id=((xx // 2) * 4 + zz, xx % 2, yy * 2 + cc), device_id_type=MESH
        )

    greet(z, y, x, 1 - core)
    for i in range(1, 4):
        for cc in range(2):
            greet(z, (y + i) % 4, x, cc)
            greet((z + i) % 4, y, x, cc)
    for i in range(4):
        for k in range(1, 4):
            gg = (g + i) % 4
            greet(gg * (1 - core) + z * core, y * (1 - core) + gg * core, (x + k) % 4, core)
    pl.semaphore_wait(barrier, 25)

    myb = g * 2 + xh
    rts[myb] = rt[...]

    def at_tsg(t):
        return at_gx(t % 4, (t // 4) * 2 + dp)

    def rt_copy(i):
        return remote(rt, rts.at[myb], rt_ss.at[i - 1], rt_rs.at[i - 1], at_tsg((tsg + i) % 8))

    for i in range(1, 8):
        rt_copy(i).start()

    def order():
        row = lax.broadcasted_iota(jnp.int32, (EXPERTS, EXPERTS), 0)
        col = lax.broadcasted_iota(jnp.int32, (EXPERTS, EXPERTS), 1)
        turned = (row // 32) * 32 + (row // 2 % 4) * 8 + (row // 8 % 4) * 2 + row % 2
        return jnp.where(col == jnp.where(core == 0, row, turned), 1.0, 0.0).astype(BF16)

    def to_slots():
        cols8[...] = jnp.zeros_like(cols8)
        at = lax.broadcasted_iota(jnp.int32, (16, 128), 1)

        def body(d, _):
            row = rows8[pl.ds(d, 1), :]
            for k in range(MSG // 16):
                hit = pk[pl.ds(pl.multiple_of(d * MSG + k * 16, 16), 16), :].astype(F32)
                one = jnp.sum(hit * row, axis=1, keepdims=True)
                cols8[k * 16 : (k + 1) * 16, :] += jnp.where(at == d, one, 0.0)
            return 0

        lax.fori_loop(0, PEERS, body, 0)
        flat = jnp.transpose(cols8[...])
        for d in range(PEERS):
            gs[d] = flat[d : d + 1, :] + jnp.zeros((8, 256), F32)

    def to_columns(box):
        rows = [box[k][0:1, :] for k in range(PEERS)]
        cols8[...] = jnp.transpose(jnp.concatenate(rows + [jnp.zeros((120, 256), F32)], axis=0))

    def column(k, d):
        part = cols8[k * 16 : (k + 1) * 16, :]
        at = lax.broadcasted_iota(jnp.int32, (16, 128), 1)
        return jnp.sum(jnp.where(at == d, part, 0.0), axis=1, keepdims=True)

    mine = pl.multiple_of(me * TOK, TOK)
    wide = tok[...].astype(F32)
    inv = lax.rsqrt(jnp.mean(wide * wide, axis=1, keepdims=True) + 1e-06)
    u_own = (wide * inv * gain[...]).astype(BF16)
    for c in range(NC):
        xall[c, pl.ds(mine, TOK), :] = u_own[:, c * CW : (c + 1) * CW]
        xall[NC + c, pl.ds(mine, TOK), :] = dy[:, c * CW : (c + 1) * CW]

    line = pl.multiple_of(g * 4 * TOK, 4 * TOK)

    def a_copy(st, i, along_x):
        block = xall.at[st, pl.ds(mine, TOK)]
        dev = at_gx(g, (x + i) % 4) if along_x else at_gx((g + i) % 4, x)
        return remote(block, block, a_ss.at[st, i - 1], a_rs.at[st, i - 1], dev)

    def side(i, along_x):
        return at_gx(g, (x + i) % 4) if along_x else at_gx((g + i) % 4, x)

    def b_line(st, i):
        block = xall.at[st, pl.ds(line, 4 * TOK)]
        return remote(block, block, b_ss.at[st, i // 2], b_rs.at[st, i // 2], side(i, False))

    def b_piece(st, i, k):
        block = xall.at[st, pl.ds(pl.multiple_of((k * 4 + x) * TOK, TOK), TOK)]
        return remote(block, block, b_ss.at[st, i // 2], b_rs.at[st, i // 2], side(i, True))

    def f_line(st, i):
        at = (g - i + 4) % 4 * 4 * TOK + (i // 2) * 2 * TOK
        block = xall.at[st, pl.ds(pl.multiple_of(at, TOK), 2 * TOK)]
        return remote(block, block, f_ss.at[st, i // 2], f_rs.at[st, i // 2], side(i, False))

    def f_piece(st, i, k):
        at = ((k + (i // 2) * 2) * 4 + (x - i + 4) % 4) * TOK
        block = xall.at[st, pl.ds(pl.multiple_of(at, TOK), TOK)]
        return remote(block, block, f_ss.at[st, i // 2], f_rs.at[st, i // 2], side(i, True))

    def first(st):
        for i in (1, 3, 2):
            a_copy(st, i, st == 0).start()

    def forward(st):
        for i in (1, 3, 2):
            a_copy(st, i, True).wait_recv()

        @pl.when(st == 0)
        def _():
            for i in (1, 3):
                b_line(st, i).start()

        @pl.when(st != 0)
        def _():
            for i in (1, 3):
                for k in range(4):
                    b_piece(st, i, k).start()

    def onward(st):
        for i in (1, 3):
            b_line(st, i).wait_recv()

            @pl.when(st == 0)
            def _():
                f_line(st, i).start()

            @pl.when(st != 0)
            def _():
                for k in range(2):
                    f_piece(st, i, k).start()

    for st in range(4):
        first(st)
    forward(0)
    forward(1)
    forward(2)
    for st in range(4, 2 * NC):
        first(st)
    for i in range(1, 8):
        rt_copy(i).wait_recv()
    lane = lax.broadcasted_iota(jnp.int32, (128, 128), 1)
    sub = lax.broadcasted_iota(jnp.int32, (128, 128), 0)
    before = jnp.where((sub < lane) & ((sub // TOK) == (lane // TOK)), 1.0, 0.0).astype(BF16)
    for b in range(8):
        r = rts[b]
        ids = lax.broadcasted_iota(jnp.int32, (16, 128), 0)
        own = jnp.zeros((16, 128), F32)
        for k in range(6):
            own = own + jnp.where((r[k : k + 1, :] == tsg * PEERS + ids) & (ids < PEERS), 1.0, 0.0)
        rank = dot(own.astype(BF16), before)
        half = lax.broadcasted_iota(jnp.int32, (16, 128), 1) // TOK
        slot = jnp.where(own > 0.5, (2 * b + half) * MOST + rank.astype(jnp.int32), -1)
        slots[:, b * 128 : (b + 1) * 128] = slot

    def slot_body(d, _):
        row = slots[pl.ds(d, 1), :]
        hit = lax.broadcasted_iota(jnp.int32, (MSG, ALL), 0) == row
        pk[pl.ds(pl.multiple_of(d * MSG, MSG), MSG), :] = jnp.where(hit, 1.0, 0.0).astype(BF16)
        return 0

    lax.fori_loop(0, PEERS, slot_body, 0)
    onward(0)
    def d_copy(st, d):
        return remote(
            send.at[st % NC, rows_of(d)], rall.at[st, rows_of(seat)], d_ss.at[st, d], d_rs.at[st, seat], at_dest(d)
        )

    def d_arrival(st, e):
        return remote(send.at[st % NC, rows_of(e)], rall.at[st, rows_of(e)], d_ss.at[st, e], d_rs.at[st, e], at_src(e))

    def own_copy(st):
        return pltpu.make_async_copy(send.at[st % NC, rows_of(own_d)], rall.at[st, rows_of(seat)], lsem.at[st])

    def pack(st):
        for i in (1, 3):
            f_line(st, i).wait_recv()

        def body(i, _):
            bb = (b_at + 1 + i) % 4
            rows = pl.ds(pl.multiple_of(bb * 2 * MSG, 2 * MSG), 2 * MSG)
            send[st % NC, rows, :] = dot(pk[rows, :], xall[st, pl.ds(0, ALL), :]).astype(BF16)
            for cc in range(2):
                d = bb * 2 + cc

                @pl.when(d != own_d)
                def _():
                    d_copy(st, d).start()

            return 0

        lax.fori_loop(0, 4, body, 0)
        own_copy(st).start()

        @pl.when(st + 1 < 2 * NC)
        def _():
            onward(st + 1)

    def gathered(st):
        for i in (1, 3, 2):
            a_copy(st, i, True).wait_send()
        for i in (1, 3):
            b_line(st, i).wait_send()
            f_line(st, i).wait_send()

    def u_body(c, _):
        forward(c + 3)
        pack(c)
        rw = dot(order(), rw_in[:, pl.ds(pl.multiple_of(c * CW, CW), CW)]).astype(BF16)
        part = dot(rw, xall[c, pl.ds(0, ALL), :], NT)

        @pl.when(c == 0)
        def _():
            zt[...] = part

        @pl.when(c > 0)
        def _():
            zt[...] += part

        return 0

    lax.fori_loop(0, NC, u_body, 0)

    for b in range(8):
        lanes = slice(b * 128, (b + 1) * 128)
        r = rts[b]
        ids = lax.broadcasted_iota(jnp.int32, (EXPERTS, 128), 0)
        mask = jnp.zeros((EXPERTS, 128), F32)
        for k in range(6):
            mask = mask + jnp.where(r[k : k + 1, :] == ids, 1.0, 0.0)
        sg = jax.nn.sigmoid(zt[:, lanes])
        zt[:, lanes] = sg
        rowg[:, lanes] = jnp.sum(mask * sg, axis=0, keepdims=True)
    gt = (zt[pl.ds(pl.multiple_of(tsg * PEERS, PEERS), PEERS), :] / rowg[...]).astype(BF16)

    def g_copy(d):
        return remote(gs.at[d], gr.at[seat], g_ss.at[d], g_rs.at[seat], at_dest(d))

    def g_arrival(e):
        return remote(gs.at[e], gr.at[e], g_ss.at[e], g_rs.at[e], at_src(e))

    rows8[...] = gt.astype(F32)
    to_slots()
    gr[seat] = gs[own_d]
    others(own_d, lambda d: g_copy(d).start())

    def wait_d(st):
        others(seat, lambda e: d_arrival(st, e).wait_recv())
        own_copy(st).wait()

    NTILE = ROWS // 3

    def ab_body(c, _):
        others(own_d, lambda d: d_copy(c, d).wait_send())

        @pl.when(c + 3 < NC)
        def _():
            forward(NC + c + 3)

        wait_d(c)
        gathered(c)
        pack(NC + c)
        for i in range(2):
            wcopy_dyn(i, c).wait()

        def tile(t, _):
            cols = pl.ds(pl.multiple_of(t * NTILE, NTILE), NTILE)
            rows = rall[c, cols, :]
            pa = dot(wg[c], rows, NT)
            pb = dot(wu[c], rows, NT)

            @pl.when(c == 0)
            def _():
                acc1[:, cols] = pa
                acc2[:, cols] = pb

            @pl.when(c > 0)
            def _():
                acc1[:, cols] += pa
                acc2[:, cols] += pb

            return 0

        lax.fori_loop(0, 3, tile, 0)
        return 0

    def wcopy_dyn(i, c):
        src, dst = ((wg_in, wg), (wu_in, wu), (wd_in, wd))[i]
        return pltpu.make_async_copy(
            src.at[:, pl.ds(pl.multiple_of(c * CW, CW), CW)], dst.at[c], wsem.at[i, c]
        )

    lax.fori_loop(0, NC, ab_body, 0)

    def drain(st, _):
        gathered(st)
        return 0

    lax.fori_loop(NC, 2 * NC, drain, 0)
    for i in range(1, 4):
        for dev in (at_gx((g + i) % 4, x), at_gx(g, (x + i) % 4)):
            pl.semaphore_signal(free_sem.at[0], inc=1, device_id=dev, device_id_type=MESH)

    FT = 32

    def act_body(t, _):
        f = pl.ds(pl.multiple_of(t * FT, FT), FT)
        a, b = acc1[f, :], acc2[f, :]
        sg = jax.nn.sigmoid(a)
        act = a * sg
        h[f, :] = (act * b).astype(BF16)
        s[f, :] = act.astype(BF16)
        q[f, :] = (b * sg * (1.0 + a * (1.0 - sg))).astype(BF16)
        return 0

    lax.fori_loop(0, SH // FT, act_body, 0)

    others(seat, lambda e: g_arrival(e).wait_recv())
    total = jnp.zeros((8, ROWS + 128), F32)
    zpad = jnp.zeros((8, ROWS + 128 - 256), F32)
    for e in range(PEERS):
        piece = jnp.concatenate([gr[e], zpad], axis=1)
        total = total + (pltpu.roll(piece, e * MSG, 1) if e else piece)
    gwrow[...] = total[:, 0:ROWS]

    def p_body(c, _):
        wait_d(NC + c)
        wcopy_dyn(2, c).wait()

        def tile(t, _):
            cols = pl.ds(pl.multiple_of(t * NTILE, NTILE), NTILE)
            pp = dot(wd[c], rall[NC + c, cols, :], NT)

            @pl.when(c == 0)
            def _():
                acc1[:, cols] = pp

            @pl.when(c > 0)
            def _():
                acc1[:, cols] += pp

            return 0

        lax.fori_loop(0, 3, tile, 0)
        return 0

    lax.fori_loop(0, NC, p_body, 0)

    dgrow[...] = jnp.zeros_like(dgrow)
    GT = 128

    def grad_body(t, _):
        f = pl.ds(pl.multiple_of(t * GT, GT), GT)
        part = jnp.zeros((8, ROWS), F32)
        gw = gwrow[0:1, :]
        for k in range(GT // 16):
            fk = pl.ds(pl.multiple_of(t * GT + k * 16, 16), 16)
            p = acc1[fk, :]
            hh = h[fk, :].astype(F32)
            prod = hh * p
            part = part + prod[0:8] + prod[8:16]
            dh = p * gw
            q[fk, :] = (dh * q[fk, :].astype(F32)).astype(BF16)
            s[fk, :] = (dh * s[fk, :].astype(F32)).astype(BF16)
            h[fk, :] = (hh * gw).astype(BF16)
        dgrow[...] += part
        da[:, f] = jnp.transpose(q[f, :])
        db[:, f] = jnp.transpose(s[f, :])
        return 0

    lax.fori_loop(0, SH // GT, grad_body, 0)

    def dg_copy(e):
        return remote(ds_.at[e], dr.at[d_at(e)], dg_ss.at[e], dg_rs.at[d_at(e)], at_src(e))

    def dg_arrival(d):
        return remote(ds_.at[d], dr.at[d], dg_ss.at[d], dg_rs.at[d], at_dest(d))

    dg = jnp.sum(dgrow[...], axis=0, keepdims=True) + jnp.zeros((8, ROWS), F32)
    dg = jnp.concatenate([dg, jnp.zeros((8, 128), F32)], axis=1)
    keep = lax.broadcasted_iota(jnp.int32, (8, 256), 1) < MSG
    for e in range(PEERS):
        moved = pltpu.roll(dg, ROWS + 128 - e * MSG, 1) if e else dg
        ds_[e] = jnp.where(keep, moved[:, 0:256], 0.0)
    dr[own_d] = ds_[seat]
    others(seat, lambda e: dg_copy(e).start())

    def ret_copy(c, e):
        return remote(
            send.at[c, rows_of(e)], xall.at[c, rows_of(d_at(e))], r_ss.at[c, e], r_rs.at[c, d_at(e)], at_src(e)
        )

    def ret_arrival(c, d):
        return remote(send.at[c, rows_of(d)], xall.at[c, rows_of(d)], r_ss.at[c, d], r_rs.at[c, d], at_dest(d))

    def own_ret(c):
        return pltpu.make_async_copy(send.at[c, rows_of(seat)], xall.at[c, rows_of(own_d)], lsem.at[c])

    def ret_body(c, _):
        others(own_d, lambda d: d_copy(NC + c, d).wait_send())

        def body(i, _):
            m = (seat // 2 + 1 + i) % 4
            rows = pl.ds(pl.multiple_of(m * 2 * MSG, 2 * MSG), 2 * MSG)
            send[c, rows, :] = (dot(da[rows, :], wg[c]) + dot(db[rows, :], wu[c])).astype(BF16)
            for cc in range(2):
                e = m * 2 + cc

                @pl.when(e != seat)
                def _():
                    ret_copy(c, e).start()

            return 0

        lax.fori_loop(0, 4, body, 0)
        own_ret(c).start()
        return 0

    def out_copy(i, c):
        src, dst = ((wg, gg_out), (wu, gu_out), (wd, gd_out))[i]
        return pltpu.make_async_copy(
            src.at[c], dst.at[:, pl.ds(pl.multiple_of(c * CW, CW), CW)], osem.at[i, c]
        )

    MT = 256

    def wgrad_body(c, _):
        gaccum[c] = jnp.zeros((8, CW), F32)

        def tile(t, _):
            f = pl.ds(pl.multiple_of(t * MT, MT), MT)
            ga = dot(q[f, :], rall[c])
            part = jnp.sum(ga * wg[c, f, :].astype(F32), axis=0, keepdims=True)
            wg[c, f, :] = ga.astype(BF16)
            gb = dot(s[f, :], rall[c])
            part = part + jnp.sum(gb * wu[c, f, :].astype(F32), axis=0, keepdims=True)
            wu[c, f, :] = gb.astype(BF16)
            gaccum[c] += part + jnp.zeros((8, CW), F32)
            wd[c, f, :] = dot(h[f, :], rall[NC + c]).astype(BF16)
            return 0

        lax.fori_loop(0, SH // MT, tile, 0)
        for i in range(3):
            out_copy(i, c).start()
        return 0

    ret_body(0, 0)

    def dt_copy(i):
        p = (me + i) % SRC
        gg, xx = p // 4, p % 4
        return remote(dgt.at[gg * 2 + xx // 2], dgr.at[me], dt_ss.at[i - 1], dt_rs.at[i - 1], at_gx(gg, xx))

    others(own_d, lambda d: dg_arrival(d).wait_recv())
    to_columns(dr)

    def dgt_body(d, _):
        got = jnp.zeros((1, ALL), F32)
        for k in range(MSG // 16):
            hit = pk[pl.ds(pl.multiple_of(d * MSG + k * 16, 16), 16), :].astype(F32)
            got = got + jnp.sum(hit * column(k, d), axis=0, keepdims=True)
        for b in range(8):
            dgt[b, pl.ds(d, 1), :] = got[:, b * 128 : (b + 1) * 128]
        return 0

    lax.fori_loop(0, PEERS, dgt_body, 0)
    dgr[me] = dgt[myb]
    for i in range(1, SRC):
        dt_copy(i).start()

    ret_body(1, 0)

    for i in range(1, SRC):
        dt_copy(i).wait_recv()
    for t in range(8):
        zz, hh = t % 4, t // 4
        j = zz * 4 + hh * 2
        dzs[t * 8 : (t + 1) * 8, :] = dgr[j] + dgr[j + 1]
    lanes = pl.ds(pl.multiple_of(myb * 128, 128), 128)
    r = rt[...]
    ids = lax.broadcasted_iota(jnp.int32, (EXPERTS, 128), 0)
    mask = jnp.zeros((EXPERTS, 128), F32)
    for k in range(6):
        mask = mask + jnp.where(r[k : k + 1, :] == ids, 1.0, 0.0)
    sg = zt[:, lanes]
    tot = rowg[0:1, lanes]
    dg = dzs[...]
    mixed = jnp.sum(mask * (sg / tot) * dg, axis=0, keepdims=True)
    dzs[...] = mask * ((dg - mixed) / tot) * sg * (1.0 - sg)

    def zb_copy(i):
        t = (tsg + i) % 8
        return remote(
            dzs.at[pl.ds(pl.multiple_of(t * 8, 8), 8)], dgt.at[myb], zb_ss.at[i - 1], zb_rs.at[i - 1], at_tsg(t)
        )

    for i in range(1, SRC):
        dt_copy(i).wait_send()
    dgt[myb] = dzs[pl.ds(pl.multiple_of(tsg * 8, 8), 8), :]
    for i in range(1, 8):
        pl.semaphore_signal(free_sem.at[1], inc=1, device_id=at_tsg((tsg + i) % 8), device_id_type=MESH)
    pl.semaphore_wait(free_sem.at[1], 7)
    for i in range(1, 8):
        zb_copy(i).start()

    lax.fori_loop(2, NC - 1, ret_body, 0)

    def zs_copy(d):
        return remote(gs.at[d], zr.at[seat], zs_ss.at[d], zs_rs.at[seat], at_dest(d))

    def zs_arrival(e):
        return remote(gs.at[e], zr.at[e], zs_ss.at[e], zs_rs.at[e], at_src(e))

    for i in range(1, 8):
        zb_copy(i).wait_recv()
    others(own_d, lambda d: g_copy(d).wait_send())
    for b in range(8):
        rows8[:, b * 128 : (b + 1) * 128] = dgt[b]
    to_slots()
    zr[seat] = gs[own_d]
    others(own_d, lambda d: zs_copy(d).start())
    ret_body(NC - 1, 0)

    for b in range(8):
        lanes = slice(b * 128, (b + 1) * 128)
        da[lanes, 0:KA] = jnp.transpose(pk[0:KA, lanes])
        db[lanes, 0:KB] = jnp.transpose(pk[KA:ROWS, lanes])

    def p1_rows(d):
        return acc2.at[pl.ds(pl.multiple_of(d * 48, 8), 48), pl.ds(0, 128)]

    def p1_copy(e):
        return remote(row_s, p1_rows(d_at(e)), p1_ss.at[e], p1_rs.at[d_at(e)], at_src(e))

    def p1_arrival(d):
        return remote(row_s, p1_rows(d), p1_ss.at[d], p1_rs.at[d], at_dest(d))

    def router_row():
        others(seat, lambda e: zs_arrival(e).wait_recv())
        to_columns(zr)
        rrow[...] = jnp.zeros_like(rrow)

        def body(e, _):
            for k in range(MSG // 16):
                one = column(k, e)
                for c in range(NC):
                    rows = rall[c, pl.ds(pl.multiple_of(e * MSG + k * 16, 16), 16), :].astype(F32) * one
                    rrow[c] += rows[0:8] + rows[8:16]
            return 0

        lax.fori_loop(0, PEERS, body, 0)
        for c in range(NC):
            row = jnp.sum(rrow[c], axis=0, keepdims=True)
            part = gaccum[c]
            for j in range(CW // 128):
                n = c * (CW // 128) + j
                row_s[n : n + 1, :] = row[:, j * 128 : (j + 1) * 128]
                row_s[24 + n : 25 + n, :] = part[0:1, j * 128 : (j + 1) * 128]
        others(seat, lambda e: p1_copy(e).start())
        acc2[pl.ds(pl.multiple_of(own_d * 48, 8), 48), 0:128] = row_s[...]

    def grt(c, k, n):
        return acc2.at[pl.ds(pl.multiple_of(c * EXPERTS + k * 8, 8), 8 * n), pl.ds(256, CW)]

    def p2_copy(i, c):
        block = grt(c, tsg, 1)
        return remote(block, block, p2_ss.at[i - 1], p2_rs.at[i - 1], at_tsg((tsg + i) % 8))

    def p2_all(i):
        block = grt(0, 0, NC)
        return remote(block, block, p2_ss.at[i - 1], p2_rs.at[i - 1], at_tsg((tsg + i) % 8))

    mygain = pl.ds(pl.multiple_of(me * 24, 8), 24)

    def p3_copy(i):
        p = (me + i) % SRC
        block = acc2.at[mygain, pl.ds(128, 128)]
        return remote(block, block, p3_ss.at[i - 1], p3_rs.at[i - 1], at_gx(p // 4, p % 4))

    def router_rows():
        others(own_d, lambda d: p1_arrival(d).wait_recv())
        for n in range(D // 128):
            rows = [acc2[e * 48 + n : e * 48 + n + 1, 0:128] for e in range(PEERS)]
            c, o = n * 128 // CW, 256 + n * 128 % CW
            at = pl.ds(pl.multiple_of(c * EXPERTS + tsg * 8, 8), 8)
            acc2[at, o : o + 128] = jnp.concatenate(rows, axis=0)
        tot = acc2[24:48, 0:128]
        for e in range(1, PEERS):
            tot = tot + acc2[e * 48 + 24 : (e + 1) * 48, 0:128]
        acc2[mygain, 128:256] = tot
        for i in range(1, 8):
            for c in range(NC):
                p2_copy(i, c).start()
        for i in range(1, SRC):
            p3_copy(i).start()

    pl.semaphore_wait(free_sem.at[0], 6)


    def z_line(c, i):
        gg = (g + i) % 4
        return remote(
            send.at[c, pl.ds(pl.multiple_of(gg * 4 * TOK, 4 * TOK), 4 * TOK)],
            xall.at[NC + c, pl.ds((i - 1) * 4 * TOK, 4 * TOK)],
            z_ss.at[c, i - 1],
            z_rs.at[c, i - 1],
            at_gx(gg, x),
        )

    def z_piece(c, i, k):
        xx = (x + i) % 4
        return remote(
            send.at[c, pl.ds(pl.multiple_of((k * 4 + xx) * TOK, TOK), TOK)],
            xall.at[NC + c, pl.ds(pl.multiple_of((i - 1) * 4 * TOK + k * TOK, TOK), TOK)],
            z_ss.at[c, i - 1],
            z_rs.at[c, i - 1],
            at_gx(g, xx),
        )

    def x_copy(c, i, along_x):
        xx, gg = ((x + i) % 4, g) if along_x else (x, (g + i) % 4)
        return remote(
            send.at[c, pl.ds(pl.multiple_of((gg * 4 + xx) * TOK, TOK), TOK)],
            xall.at[NC + c, pl.ds(12 * TOK + (i - 1) * TOK, TOK)],
            x_ss.at[c, i - 1],
            x_rs.at[c, i - 1],
            at_gx(gg, xx),
        )

    def comb_body(c):
        others(own_d, lambda d: ret_arrival(c, d).wait_recv())
        others(seat, lambda e: ret_copy(c, e).wait_send())
        own_ret(c).wait()

        def body(i, _):
            gg = (g + 1 + i) % 4
            rows = pl.ds(pl.multiple_of(gg * 4 * TOK, 4 * TOK), 4 * TOK)
            low = dot(da[rows, 0:KA], xall[c, 0:KA, :])
            send[c, rows, :] = (low + dot(db[rows, 0:KB], xall[c, KA:ROWS, :])).astype(BF16)

            @pl.when((i < 3) & (c >= 2))
            def _():
                z_line(c, i + 1).start()

            @pl.when(c < 2)
            def _():
                for k in (1, 3, 2):
                    z_piece(c, k, gg).start()

            return 0

        lax.fori_loop(0, 4, body, 0)

    def z_sum(c):
        for i in (1, 3, 2):
            z_line(c, i).wait_recv()

        def body(k, _):
            row = jnp.where(c >= 2, g * 4 + k, k * 4 + x) * TOK
            rows = pl.ds(pl.multiple_of(row, TOK), TOK)
            tot = send[c, rows, :].astype(F32)
            for i in range(3):
                part = pl.ds(pl.multiple_of((i * 4 + k) * TOK, TOK), TOK)
                tot = tot + xall[NC + c, part, :].astype(F32)
            send[c, rows, :] = tot.astype(BF16)
            return 0

        lax.fori_loop(0, 4, body, 0)

        @pl.when(c >= 2)
        def _():
            for i in (1, 3, 2):
                x_copy(c, i, True).start()

        @pl.when(c < 2)
        def _():
            for i in (1, 3, 2):
                x_copy(c, i, False).start()

    comb_body(0)
    wgrad_body(0, 0)
    comb_body(1)
    z_sum(0)
    lax.fori_loop(1, 3, wgrad_body, 0)
    comb_body(2)
    z_sum(1)
    wgrad_body(3, 0)
    router_row()
    comb_body(3)
    z_sum(2)
    router_rows()
    z_sum(3)

    pad = jnp.concatenate([dzs[...], jnp.zeros((64, 128), F32)], axis=0)
    acc1[0:128, 0:128] = jnp.transpose(pad)
    dz_own = acc1[pl.ds(pl.multiple_of(dp * TOK, TOK), TOK), 0:EXPERTS]
    hi, lo = split(dz_own)
    both = dot(jnp.concatenate([hi, lo], axis=0), order()).astype(BF16)
    for c in range(NC):
        cols = slice(c * CW, (c + 1) * CW)
        two = dot(both, rw_in[:, cols])
        gx_out[:, cols] = two[0:TOK] + two[TOK : 2 * TOK]
    wide = tok[...].astype(F32)
    inv = lax.rsqrt(jnp.mean(wide * wide, axis=1, keepdims=True) + 1e-06)

    for i in range(1, 8):
        p2_all(i).wait_recv()
    for i in range(1, SRC):
        p3_copy(i).wait_recv()
    tot = acc2[0:24, 128:256]
    for p in range(1, SRC):
        tot = tot + acc2[p * 24 : (p + 1) * 24, 128:256]
    thrice = jnp.concatenate([order()] * 3, axis=1)
    for c in range(NC):
        rest = acc2[c * EXPERTS : (c + 1) * EXPERTS, 256 : 256 + CW]
        parts = []
        for _ in range(3):
            hi, rest = split32(rest)
            parts.append(hi)
        gr_out[:, c * CW : (c + 1) * CW] = dot(thrice, jnp.concatenate(parts, axis=0))
    for n in range(D // 128):
        cols = slice(n * 128, (n + 1) * 128)
        along = jnp.sum(gr_out[:, cols] * rw_in[:, cols].astype(F32), axis=0, keepdims=True)
        gn_out[:, cols] = (along + tot[n : n + 1, :]) / gain[:, cols]

    for c in range(NC):
        cols = slice(c * CW, (c + 1) * CW)
        du = gx_out[:, cols]
        for i in (1, 3, 2):
            x_copy(c, i, True).wait_recv()
        du = du + send[c, pl.ds(mine, TOK), :].astype(F32)
        for i in range(3):
            du = du + xall[NC + c, (12 + i) * TOK : (13 + i) * TOK, :].astype(F32)
        gx_out[:, cols] = du * gain[:, cols]
    v = wide * inv
    scaled = gx_out[...]
    gx_out[...] = inv * scaled - v * inv * jnp.mean(v * scaled, axis=1, keepdims=True)

    def drain2(c, _):
        for i in (1, 3, 2):
            z_line(c, i).wait_send()
            x_copy(c, i, True).wait_send()
        for i in range(3):
            out_copy(i, c).wait()
        return 0

    lax.fori_loop(0, NC, drain2, 0)
    for i in range(1, 8):
        rt_copy(i).wait_send()
        zb_copy(i).wait_send()
        p2_all(i).wait_send()
    others(own_d, lambda d: zs_copy(d).wait_send())
    others(seat, lambda e: dg_copy(e).wait_send())
    others(seat, lambda e: p1_copy(e).wait_send())
    for i in range(1, SRC):
        p3_copy(i).wait_send()


def call(tok, dy, rt, gain, rwt, wg, wu, wd):
    vmem = pl.BlockSpec(memory_space=pltpu.VMEM)
    hbm = pl.BlockSpec(memory_space=pl.ANY)
    V = pltpu.VMEM
    S = pltpu.SemaphoreType.DMA
    weight = jax.ShapeDtypeStruct((SH, D), BF16)
    return pl.pallas_call(
        kernel,
        out_shape=(
            jax.ShapeDtypeStruct((TOK, D), F32),
            jax.ShapeDtypeStruct((EXPERTS, D), F32),
            jax.ShapeDtypeStruct((1, D), F32),
            weight, weight, weight,
        ),
        in_specs=[vmem] * 5 + [hbm] * 3,
        out_specs=(vmem, vmem, vmem, hbm, hbm, hbm),
        scratch_shapes=[
            V((2 * NC, ROWS, CW), BF16),
            V((2 * NC, ROWS, CW), BF16),
            V((NC, ROWS, CW), BF16),
            V((NC, SH, CW), BF16), V((NC, SH, CW), BF16), V((NC, SH, CW), BF16),
            V((SH, ROWS), F32), V((SH, ROWS), F32),
            V((SH, ROWS), BF16), V((SH, ROWS), BF16), V((SH, ROWS), BF16),
            V((ROWS, SH), BF16), V((ROWS, SH), BF16),
            V((ROWS, ALL), BF16),
            V((8, 8, 128), jnp.int32),
            V((EXPERTS, ALL), F32),
            V((16, ALL), jnp.int32),
            V((8, 8, 256), F32), V((8, 8, 256), F32),
            V((8, 8, 256), F32), V((8, 8, 256), F32),
            V((8, 8, 128), F32), V((SRC, 8, 128), F32),
            V((8, ROWS), F32), V((8, ROWS), F32),
            V((1, ALL), F32), V((EXPERTS, 128), F32),
            V((NC, 8, CW), F32), V((8, 8, 256), F32), V((48, 128), F32), V((8, ALL), F32), V((256, 128), F32), V((NC, 8, CW), F32),
            S((3, NC)), S((3, NC)), S((2 * NC,)),
            S((7,)), S((7,)),
            S((2 * NC, 3)), S((2 * NC, 3)), S((2 * NC, 2)), S((2 * NC, 2)), S((2 * NC, 2)), S((2 * NC, 2)),
            S((2 * NC, 8)), S((2 * NC, 8)),
            S((8,)), S((8,)), S((8,)), S((8,)),
            S((15,)), S((15,)),
            S((NC, 8)), S((NC, 8)),
            S((NC, 3)), S((NC, 3)), S((NC, 3)), S((NC, 3)),
            S((7,)), S((7,)), S((8,)), S((8,)), S((8,)), S((8,)),
            S((7,)), S((7,)), S((15,)), S((15,)),
            pltpu.SemaphoreType.REGULAR((2,)),
        ],
        compiler_params=pltpu.CompilerParams(
            collective_id=0, has_side_effects=True, vmem_limit_bytes=VMEM_LIMIT
        ),
    )(tok, dy, rt, gain, rwt, wg, wu, wd)


VMEM_LIMIT = 65472 * 1024


def local(tokens, out_grad, routes, norm_gain, router_w, w_gate, w_up, w_down):
    core = lax.axis_index("ep") % 2
    ids = routes[0].T
    turned = (ids // 32) * 32 + (ids // 2 % 4) * 8 + (ids // 8 % 4) * 2 + ids % 2
    rt = jnp.pad(jnp.where(core == 0, ids, turned), ((0, 2), (0, 0)), constant_values=-1)
    gain = norm_gain.astype(F32)[None]

    gx, grt, gn, gg, gu, gd = call(
        tokens[0], out_grad[0], rt, gain, router_w.T, w_gate[0], w_up[0], w_down[0]
    )
    return (gx[None], gg[None], gu[None], gd[None], grt.T, gn[0])


def solution(mesh):
    split3 = P(("ts", "ep"), "dp", None)
    return jax.shard_map(
        local,
        mesh=mesh,
        in_specs=(split3, split3, P(("ts", "ep"), None, None), P(), P(), split3, split3, split3),
        out_specs=(split3, split3, split3, split3, P(), P()),
        check_vma=False,
    )
```

```python
import jax
import jax.numpy as jnp
from jax import lax
from jax.experimental import pallas as pl
from jax.experimental.pallas import tpu as pltpu
from jax.sharding import PartitionSpec as P

MESH = pl.DeviceIdType.MESH
F32 = jnp.float32
BF16 = jnp.bfloat16
D = 2560
NC = 5
CW = D // NC
TOK = 64
MOST = 9
SRC = 16
MSG = SRC * MOST
PEERS = 8
ROWS = PEERS * MSG
ALL = SRC * TOK
SH = 768
EXPERTS = 64
KA = 640
KB = ROWS - KA
NT = (((1,), (1,)), ((), ()))
TN = (((0,), (0,)), ((), ()))


def dot(a, b, dims=(((1,), (0,)), ((), ()))):
    return lax.dot_general(a, b, dims, preferred_element_type=F32)


def split(a):
    hi = a.astype(BF16)
    return hi, (a - hi.astype(F32)).astype(BF16)


def split32(a):
    hi = a.astype(BF16)
    return hi, a - hi.astype(F32)


def kernel(
    tok, dy, rt, gain, rw_in, wg_in, wu_in, wd_in,
    gx_out, gr_out, gn_out, gg_out, gu_out, gd_out,
    xall, rall, send, wg, wu, wd, acc1, acc2, q, s, h, da, db, pk,
    rts, zt, slots, gs, gr, ds_, dr, dgt, dzt, dgr, gwrow, dgrow, rowg, dzs, gaccum, zr, row_s, rows8, cols8, rrow,
    wsem, osem, lsem,
    rt_ss, rt_rs, a_ss, a_rs, b_ss, b_rs, f_ss, f_rs, d_ss, d_rs, g_ss, g_rs, dg_ss, dg_rs, dt_ss, dt_rs,
    r_ss, r_rs, z_ss, z_rs, x_ss, x_rs, zb_ss, zb_rs, zs_ss, zs_rs, p1_ss, p1_rs, p2_ss, p2_rs, p3_ss, p3_rs, free_sem,
):
    ts, dp, ep = lax.axis_index("ts"), lax.axis_index("dp"), lax.axis_index("ep")
    xh, z = ts // 4, ts % 4
    x = xh * 2 + dp
    y, core = ep // 2, ep % 2
    g = z * (1 - core) + y * core
    b_at = y * (1 - core) + z * core
    me = g * 4 + x
    tsg = xh * 4 + g
    seat = core * 4 + b_at
    own_d = b_at * 2 + core

    def at_gx(gg, xx):
        zz = gg * (1 - core) + z * core
        yy = y * (1 - core) + gg * core
        return ((xx // 2) * 4 + zz, xx % 2, yy * 2 + core)

    def at_dest(d):
        bb = d // 2
        zz = z * (1 - core) + bb * core
        yy = bb * (1 - core) + y * core
        return (xh * 4 + zz, dp, yy * 2 + d % 2)

    def at_src(e):
        cs, bb = e // 4, e % 4
        zz = z * (1 - cs) + bb * cs
        yy = bb * (1 - cs) + y * cs
        return (xh * 4 + zz, dp, yy * 2 + cs)

    def d_at(e):
        cs = e // 4
        return (y * (1 - cs) + z * cs) * 2 + core

    def rows_of(k):
        return pl.ds(pl.multiple_of(k * MSG, MSG), MSG)

    def others(mine_, act):
        def body(k, _):
            @pl.when(k != mine_)
            def _():
                act(k)

            return 0

        lax.fori_loop(0, PEERS, body, 0)

    def remote(src, dst, ss, rs, dev):
        return pltpu.make_async_remote_copy(
            src_ref=src, dst_ref=dst, send_sem=ss, recv_sem=rs, device_id=dev, device_id_type=MESH
        )

    def wcopy(i, c):
        src, dst = ((wg_in, wg), (wu_in, wu), (wd_in, wd))[i]
        return pltpu.make_async_copy(src.at[:, pl.ds(c * CW, CW)], dst.at[c], wsem.at[i, c])

    for c in range(NC):
        for i in range(3):
            wcopy(i, c).start()

    barrier = pltpu.get_barrier_semaphore()
    def greet(zz, yy, xx, cc):
        pl.semaphore_signal(
            barrier, inc=1, device_id=((xx // 2) * 4 + zz, xx % 2, yy * 2 + cc), device_id_type=MESH
        )

    greet(z, y, x, 1 - core)
    for i in range(1, 4):
        for cc in range(2):
            greet(z, (y + i) % 4, x, cc)
            greet((z + i) % 4, y, x, cc)
    for i in range(4):
        for k in range(1, 4):
            gg = (g + i) % 4
            greet(gg * (1 - core) + z * core, y * (1 - core) + gg * core, (x + k) % 4, core)
    pl.semaphore_wait(barrier, 25)

    myb = g * 2 + xh
    rts[myb] = rt[...]

    def at_tsg(t):
        return at_gx(t % 4, (t // 4) * 2 + dp)

    def rt_copy(i):
        return remote(rt, rts.at[myb], rt_ss.at[i - 1], rt_rs.at[i - 1], at_tsg((tsg + i) % 8))

    for i in range(1, 8):
        rt_copy(i).start()

    def order():
        row = lax.broadcasted_iota(jnp.int32, (EXPERTS, EXPERTS), 0)
        col = lax.broadcasted_iota(jnp.int32, (EXPERTS, EXPERTS), 1)
        turned = (row // 32) * 32 + (row // 2 % 4) * 8 + (row // 8 % 4) * 2 + row % 2
        return jnp.where(col == jnp.where(core == 0, row, turned), 1.0, 0.0).astype(BF16)

    def to_slots():
        cols8[...] = jnp.zeros_like(cols8)
        at = lax.broadcasted_iota(jnp.int32, (16, 128), 1)

        def body(d, _):
            row = rows8[pl.ds(d, 1), :]
            for k in range(MSG // 16):
                hit = pk[pl.ds(pl.multiple_of(d * MSG + k * 16, 16), 16), :].astype(F32)
                one = jnp.sum(hit * row, axis=1, keepdims=True)
                cols8[k * 16 : (k + 1) * 16, :] += jnp.where(at == d, one, 0.0)
            return 0

        lax.fori_loop(0, PEERS, body, 0)
        flat = jnp.transpose(cols8[...])
        for d in range(PEERS):
            gs[d] = flat[d : d + 1, :] + jnp.zeros((8, 256), F32)

    def to_columns(box):
        rows = [box[k][0:1, :] for k in range(PEERS)]
        cols8[...] = jnp.transpose(jnp.concatenate(rows + [jnp.zeros((120, 256), F32)], axis=0))

    def column(k, d):
        part = cols8[k * 16 : (k + 1) * 16, :]
        at = lax.broadcasted_iota(jnp.int32, (16, 128), 1)
        return jnp.sum(jnp.where(at == d, part, 0.0), axis=1, keepdims=True)

    mine = pl.multiple_of(me * TOK, TOK)
    wide = tok[...].astype(F32)
    inv = lax.rsqrt(jnp.mean(wide * wide, axis=1, keepdims=True) + 1e-06)
    u_own = (wide * inv * gain[...]).astype(BF16)
    for c in range(NC):
        xall[c, pl.ds(mine, TOK), :] = u_own[:, c * CW : (c + 1) * CW]
        xall[NC + c, pl.ds(mine, TOK), :] = dy[:, c * CW : (c + 1) * CW]

    line = pl.multiple_of(g * 4 * TOK, 4 * TOK)

    def a_copy(st, i, along_x):
        block = xall.at[st, pl.ds(mine, TOK)]
        dev = at_gx(g, (x + i) % 4) if along_x else at_gx((g + i) % 4, x)
        return remote(block, block, a_ss.at[st, i - 1], a_rs.at[st, i - 1], dev)

    def side(i, along_x):
        return at_gx(g, (x + i) % 4) if along_x else at_gx((g + i) % 4, x)

    def b_line(st, i):
        block = xall.at[st, pl.ds(line, 4 * TOK)]
        return remote(block, block, b_ss.at[st, i // 2], b_rs.at[st, i // 2], side(i, False))

    def b_piece(st, i, k):
        block = xall.at[st, pl.ds(pl.multiple_of((k * 4 + x) * TOK, TOK), TOK)]
        return remote(block, block, b_ss.at[st, i // 2], b_rs.at[st, i // 2], side(i, True))

    def f_line(st, i):
        at = (g - i + 4) % 4 * 4 * TOK + (i // 2) * 2 * TOK
        block = xall.at[st, pl.ds(pl.multiple_of(at, TOK), 2 * TOK)]
        return remote(block, block, f_ss.at[st, i // 2], f_rs.at[st, i // 2], side(i, False))

    def f_piece(st, i, k):
        at = ((k + (i // 2) * 2) * 4 + (x - i + 4) % 4) * TOK
        block = xall.at[st, pl.ds(pl.multiple_of(at, TOK), TOK)]
        return remote(block, block, f_ss.at[st, i // 2], f_rs.at[st, i // 2], side(i, True))

    def first(st):
        for i in (1, 3, 2):
            a_copy(st, i, st == 0).start()

    def forward(st):
        for i in (1, 3, 2):
            a_copy(st, i, True).wait_recv()

        @pl.when(st == 0)
        def _():
            for i in (1, 3):
                b_line(st, i).start()

        @pl.when(st != 0)
        def _():
            for i in (1, 3):
                for k in range(4):
                    b_piece(st, i, k).start()

    def onward(st):
        for i in (1, 3):
            b_line(st, i).wait_recv()

            @pl.when(st == 0)
            def _():
                f_line(st, i).start()

            @pl.when(st != 0)
            def _():
                for k in range(2):
                    f_piece(st, i, k).start()

    for st in range(4):
        first(st)
    forward(0)
    forward(1)
    forward(2)
    for st in range(4, 2 * NC):
        first(st)
    for i in range(1, 8):
        rt_copy(i).wait_recv()
    lane = lax.broadcasted_iota(jnp.int32, (128, 128), 1)
    sub = lax.broadcasted_iota(jnp.int32, (128, 128), 0)
    before = jnp.where((sub < lane) & ((sub // TOK) == (lane // TOK)), 1.0, 0.0).astype(BF16)
    for b in range(8):
        r = rts[b]
        ids = lax.broadcasted_iota(jnp.int32, (16, 128), 0)
        own = jnp.zeros((16, 128), F32)
        for k in range(6):
            own = own + jnp.where((r[k : k + 1, :] == tsg * PEERS + ids) & (ids < PEERS), 1.0, 0.0)
        rank = dot(own.astype(BF16), before)
        half = lax.broadcasted_iota(jnp.int32, (16, 128), 1) // TOK
        slot = jnp.where(own > 0.5, (2 * b + half) * MOST + rank.astype(jnp.int32), -1)
        slots[:, b * 128 : (b + 1) * 128] = slot

    def slot_body(d, _):
        row = slots[pl.ds(d, 1), :]
        hit = lax.broadcasted_iota(jnp.int32, (MSG, ALL), 0) == row
        pk[pl.ds(pl.multiple_of(d * MSG, MSG), MSG), :] = jnp.where(hit, 1.0, 0.0).astype(BF16)
        return 0

    lax.fori_loop(0, PEERS, slot_body, 0)
    onward(0)
    def d_copy(st, d):
        return remote(
            send.at[st % NC, rows_of(d)], rall.at[st, rows_of(seat)], d_ss.at[st, d], d_rs.at[st, seat], at_dest(d)
        )

    def d_arrival(st, e):
        return remote(send.at[st % NC, rows_of(e)], rall.at[st, rows_of(e)], d_ss.at[st, e], d_rs.at[st, e], at_src(e))

    def own_copy(st):
        return pltpu.make_async_copy(send.at[st % NC, rows_of(own_d)], rall.at[st, rows_of(seat)], lsem.at[st])

    def pack(st):
        for i in (1, 3):
            f_line(st, i).wait_recv()

        def body(i, _):
            bb = (b_at + 1 + i) % 4
            rows = pl.ds(pl.multiple_of(bb * 2 * MSG, 2 * MSG), 2 * MSG)
            send[st % NC, rows, :] = dot(pk[rows, :], xall[st, pl.ds(0, ALL), :]).astype(BF16)
            for cc in range(2):
                d = bb * 2 + cc

                @pl.when(d != own_d)
                def _():
                    d_copy(st, d).start()

            return 0

        lax.fori_loop(0, 4, body, 0)
        own_copy(st).start()

        @pl.when(st + 1 < 2 * NC)
        def _():
            onward(st + 1)

    def gathered(st):
        for i in (1, 3, 2):
            a_copy(st, i, True).wait_send()
        for i in (1, 3):
            b_line(st, i).wait_send()
            f_line(st, i).wait_send()

    def u_body(c, _):
        forward(c + 3)
        pack(c)
        rw = dot(order(), rw_in[:, pl.ds(pl.multiple_of(c * CW, CW), CW)]).astype(BF16)
        part = dot(rw, xall[c, pl.ds(0, ALL), :], NT)

        @pl.when(c == 0)
        def _():
            zt[...] = part

        @pl.when(c > 0)
        def _():
            zt[...] += part

        return 0

    lax.fori_loop(0, NC, u_body, 0)

    for b in range(8):
        lanes = slice(b * 128, (b + 1) * 128)
        r = rts[b]
        ids = lax.broadcasted_iota(jnp.int32, (EXPERTS, 128), 0)
        mask = jnp.zeros((EXPERTS, 128), F32)
        for k in range(6):
            mask = mask + jnp.where(r[k : k + 1, :] == ids, 1.0, 0.0)
        sg = jax.nn.sigmoid(zt[:, lanes])
        zt[:, lanes] = sg
        rowg[:, lanes] = jnp.sum(mask * sg, axis=0, keepdims=True)
    gt = (zt[pl.ds(pl.multiple_of(tsg * PEERS, PEERS), PEERS), :] / rowg[...]).astype(BF16)

    def g_copy(d):
        return remote(gs.at[d], gr.at[seat], g_ss.at[d], g_rs.at[seat], at_dest(d))

    def g_arrival(e):
        return remote(gs.at[e], gr.at[e], g_ss.at[e], g_rs.at[e], at_src(e))

    rows8[...] = gt.astype(F32)
    to_slots()
    gr[seat] = gs[own_d]
    others(own_d, lambda d: g_copy(d).start())

    def wait_d(st):
        others(seat, lambda e: d_arrival(st, e).wait_recv())
        own_copy(st).wait()

    NTILE = ROWS // 3

    def ab_body(c, _):
        others(own_d, lambda d: d_copy(c, d).wait_send())

        @pl.when(c + 3 < NC)
        def _():
            forward(NC + c + 3)

        wait_d(c)
        gathered(c)
        pack(NC + c)
        for i in range(2):
            wcopy_dyn(i, c).wait()

        def tile(t, _):
            cols = pl.ds(pl.multiple_of(t * NTILE, NTILE), NTILE)
            rows = rall[c, cols, :]
            pa = dot(wg[c], rows, NT)
            pb = dot(wu[c], rows, NT)

            @pl.when(c == 0)
            def _():
                acc1[:, cols] = pa
                acc2[:, cols] = pb

            @pl.when(c > 0)
            def _():
                acc1[:, cols] += pa
                acc2[:, cols] += pb

            return 0

        lax.fori_loop(0, 3, tile, 0)
        return 0

    def wcopy_dyn(i, c):
        src, dst = ((wg_in, wg), (wu_in, wu), (wd_in, wd))[i]
        return pltpu.make_async_copy(
            src.at[:, pl.ds(pl.multiple_of(c * CW, CW), CW)], dst.at[c], wsem.at[i, c]
        )

    lax.fori_loop(0, NC, ab_body, 0)

    def drain(st, _):
        gathered(st)
        return 0

    lax.fori_loop(NC, 2 * NC, drain, 0)
    for i in range(1, 4):
        for dev in (at_gx((g + i) % 4, x), at_gx(g, (x + i) % 4)):
            pl.semaphore_signal(free_sem.at[0], inc=1, device_id=dev, device_id_type=MESH)

    FT = 32

    def act_body(t, _):
        f = pl.ds(pl.multiple_of(t * FT, FT), FT)
        a, b = acc1[f, :], acc2[f, :]
        sg = jax.nn.sigmoid(a)
        act = a * sg
        h[f, :] = (act * b).astype(BF16)
        s[f, :] = act.astype(BF16)
        q[f, :] = (b * sg * (1.0 + a * (1.0 - sg))).astype(BF16)
        return 0

    lax.fori_loop(0, SH // FT, act_body, 0)

    others(seat, lambda e: g_arrival(e).wait_recv())
    total = jnp.zeros((8, ROWS + 128), F32)
    zpad = jnp.zeros((8, ROWS + 128 - 256), F32)
    for e in range(PEERS):
        piece = jnp.concatenate([gr[e], zpad], axis=1)
        total = total + (pltpu.roll(piece, e * MSG, 1) if e else piece)
    gwrow[...] = total[:, 0:ROWS]

    def p_body(c, _):
        wait_d(NC + c)
        wcopy_dyn(2, c).wait()

        def tile(t, _):
            cols = pl.ds(pl.multiple_of(t * NTILE, NTILE), NTILE)
            pp = dot(wd[c], rall[NC + c, cols, :], NT)

            @pl.when(c == 0)
            def _():
                acc1[:, cols] = pp

            @pl.when(c > 0)
            def _():
                acc1[:, cols] += pp

            return 0

        lax.fori_loop(0, 3, tile, 0)
        return 0

    lax.fori_loop(0, NC, p_body, 0)

    dgrow[...] = jnp.zeros_like(dgrow)
    GT = 128

    def grad_body(t, _):
        f = pl.ds(pl.multiple_of(t * GT, GT), GT)
        part = jnp.zeros((8, ROWS), F32)
        gw = gwrow[0:1, :]
        for k in range(GT // 16):
            fk = pl.ds(pl.multiple_of(t * GT + k * 16, 16), 16)
            p = acc1[fk, :]
            hh = h[fk, :].astype(F32)
            prod = hh * p
            part = part + prod[0:8] + prod[8:16]
            dh = p * gw
            q[fk, :] = (dh * q[fk, :].astype(F32)).astype(BF16)
            s[fk, :] = (dh * s[fk, :].astype(F32)).astype(BF16)
            h[fk, :] = (hh * gw).astype(BF16)
        dgrow[...] += part
        da[:, f] = jnp.transpose(q[f, :])
        db[:, f] = jnp.transpose(s[f, :])
        return 0

    lax.fori_loop(0, SH // GT, grad_body, 0)

    def dg_copy(e):
        return remote(ds_.at[e], dr.at[d_at(e)], dg_ss.at[e], dg_rs.at[d_at(e)], at_src(e))

    def dg_arrival(d):
        return remote(ds_.at[d], dr.at[d], dg_ss.at[d], dg_rs.at[d], at_dest(d))

    dg = jnp.sum(dgrow[...], axis=0, keepdims=True) + jnp.zeros((8, ROWS), F32)
    dg = jnp.concatenate([dg, jnp.zeros((8, 128), F32)], axis=1)
    keep = lax.broadcasted_iota(jnp.int32, (8, 256), 1) < MSG
    for e in range(PEERS):
        moved = pltpu.roll(dg, ROWS + 128 - e * MSG, 1) if e else dg
        ds_[e] = jnp.where(keep, moved[:, 0:256], 0.0)
    dr[own_d] = ds_[seat]
    others(seat, lambda e: dg_copy(e).start())

    def ret_copy(c, e):
        return remote(
            send.at[c, rows_of(e)], xall.at[c, rows_of(d_at(e))], r_ss.at[c, e], r_rs.at[c, d_at(e)], at_src(e)
        )

    def ret_arrival(c, d):
        return remote(send.at[c, rows_of(d)], xall.at[c, rows_of(d)], r_ss.at[c, d], r_rs.at[c, d], at_dest(d))

    def own_ret(c):
        return pltpu.make_async_copy(send.at[c, rows_of(seat)], xall.at[c, rows_of(own_d)], lsem.at[c])

    def ret_body(c, _):
        others(own_d, lambda d: d_copy(NC + c, d).wait_send())

        def body(i, _):
            m = (seat // 2 + 1 + i) % 4
            rows = pl.ds(pl.multiple_of(m * 2 * MSG, 2 * MSG), 2 * MSG)
            send[c, rows, :] = (dot(da[rows, :], wg[c]) + dot(db[rows, :], wu[c])).astype(BF16)
            for cc in range(2):
                e = m * 2 + cc

                @pl.when(e != seat)
                def _():
                    ret_copy(c, e).start()

            return 0

        lax.fori_loop(0, 4, body, 0)
        own_ret(c).start()
        return 0

    def out_copy(i, c):
        src, dst = ((wg, gg_out), (wu, gu_out), (wd, gd_out))[i]
        return pltpu.make_async_copy(
            src.at[c], dst.at[:, pl.ds(pl.multiple_of(c * CW, CW), CW)], osem.at[i, c]
        )

    MT = 256

    def wgrad_body(c, _):
        gaccum[c] = jnp.zeros((8, CW), F32)

        def tile(t, _):
            f = pl.ds(pl.multiple_of(t * MT, MT), MT)
            ga = dot(q[f, :], rall[c])
            part = jnp.sum(ga * wg[c, f, :].astype(F32), axis=0, keepdims=True)
            wg[c, f, :] = ga.astype(BF16)
            gb = dot(s[f, :], rall[c])
            part = part + jnp.sum(gb * wu[c, f, :].astype(F32), axis=0, keepdims=True)
            wu[c, f, :] = gb.astype(BF16)
            gaccum[c] += part + jnp.zeros((8, CW), F32)
            wd[c, f, :] = dot(h[f, :], rall[NC + c]).astype(BF16)
            return 0

        lax.fori_loop(0, SH // MT, tile, 0)
        for i in range(3):
            out_copy(i, c).start()
        return 0

    lax.fori_loop(0, 2, ret_body, 0)

    def dt_copy(i):
        p = (me + i) % SRC
        gg, xx = p // 4, p % 4
        return remote(dgt.at[gg * 2 + xx // 2], dgr.at[me], dt_ss.at[i - 1], dt_rs.at[i - 1], at_gx(gg, xx))

    others(own_d, lambda d: dg_arrival(d).wait_recv())
    to_columns(dr)

    def dgt_body(d, _):
        got = jnp.zeros((1, ALL), F32)
        for k in range(MSG // 16):
            hit = pk[pl.ds(pl.multiple_of(d * MSG + k * 16, 16), 16), :].astype(F32)
            got = got + jnp.sum(hit * column(k, d), axis=0, keepdims=True)
        for b in range(8):
            dgt[b, pl.ds(d, 1), :] = got[:, b * 128 : (b + 1) * 128]
        return 0

    lax.fori_loop(0, PEERS, dgt_body, 0)
    dgr[me] = dgt[myb]
    for i in range(1, SRC):
        dt_copy(i).start()

    lax.fori_loop(2, NC, ret_body, 0)

    for b in range(8):
        lanes = slice(b * 128, (b + 1) * 128)
        da[lanes, 0:KA] = jnp.transpose(pk[0:KA, lanes])
        db[lanes, 0:KB] = jnp.transpose(pk[KA:ROWS, lanes])


    for i in range(1, SRC):
        dt_copy(i).wait_recv()
    for t in range(8):
        zz, hh = t % 4, t // 4
        j = zz * 4 + hh * 2
        dzs[t * 8 : (t + 1) * 8, :] = dgr[j] + dgr[j + 1]
    lanes = pl.ds(pl.multiple_of(myb * 128, 128), 128)
    r = rt[...]
    ids = lax.broadcasted_iota(jnp.int32, (EXPERTS, 128), 0)
    mask = jnp.zeros((EXPERTS, 128), F32)
    for k in range(6):
        mask = mask + jnp.where(r[k : k + 1, :] == ids, 1.0, 0.0)
    sg = zt[:, lanes]
    tot = rowg[0:1, lanes]
    dg = dzs[...]
    mixed = jnp.sum(mask * (sg / tot) * dg, axis=0, keepdims=True)
    dzs[...] = mask * ((dg - mixed) / tot) * sg * (1.0 - sg)

    def zb_copy(i):
        t = (tsg + i) % 8
        return remote(
            dzs.at[pl.ds(pl.multiple_of(t * 8, 8), 8)], dzt.at[myb], zb_ss.at[i - 1], zb_rs.at[i - 1], at_tsg(t)
        )

    dzt[myb] = dzs[pl.ds(pl.multiple_of(tsg * 8, 8), 8), :]
    for i in range(1, 8):
        zb_copy(i).start()


    def zs_copy(d):
        return remote(gs.at[d], zr.at[seat], zs_ss.at[d], zs_rs.at[seat], at_dest(d))

    def zs_arrival(e):
        return remote(gs.at[e], zr.at[e], zs_ss.at[e], zs_rs.at[e], at_src(e))

    def slots_out():
        for i in range(1, 8):
            zb_copy(i).wait_recv()
        others(own_d, lambda d: g_copy(d).wait_send())
        for b in range(8):
            rows8[:, b * 128 : (b + 1) * 128] = dzt[b]
        to_slots()
        zr[seat] = gs[own_d]
        others(own_d, lambda d: zs_copy(d).start())

    def p1_rows(d):
        return acc2.at[pl.ds(pl.multiple_of(d * 48, 8), 48), pl.ds(0, 128)]

    def p1_copy(e):
        return remote(row_s, p1_rows(d_at(e)), p1_ss.at[e], p1_rs.at[d_at(e)], at_src(e))

    def p1_arrival(d):
        return remote(row_s, p1_rows(d), p1_ss.at[d], p1_rs.at[d], at_dest(d))

    def router_row():
        others(seat, lambda e: zs_arrival(e).wait_recv())
        to_columns(zr)
        rrow[...] = jnp.zeros_like(rrow)

        def body(e, _):
            for k in range(MSG // 16):
                one = column(k, e)
                for c in range(NC):
                    rows = rall[c, pl.ds(pl.multiple_of(e * MSG + k * 16, 16), 16), :].astype(F32) * one
                    rrow[c] += rows[0:8] + rows[8:16]
            return 0

        lax.fori_loop(0, PEERS, body, 0)
        for c in range(NC):
            row = jnp.sum(rrow[c], axis=0, keepdims=True)
            part = gaccum[c]
            for j in range(CW // 128):
                n = c * (CW // 128) + j
                row_s[n : n + 1, :] = row[:, j * 128 : (j + 1) * 128]
                row_s[24 + n : 25 + n, :] = part[0:1, j * 128 : (j + 1) * 128]
        others(seat, lambda e: p1_copy(e).start())
        acc2[pl.ds(pl.multiple_of(own_d * 48, 8), 48), 0:128] = row_s[...]

    def grt(c, k, n):
        return acc2.at[pl.ds(pl.multiple_of(c * EXPERTS + k * 8, 8), 8 * n), pl.ds(256, CW)]

    def p2_copy(i, c):
        block = grt(c, tsg, 1)
        return remote(block, block, p2_ss.at[i - 1], p2_rs.at[i - 1], at_tsg((tsg + i) % 8))

    def p2_all(i):
        block = grt(0, 0, NC)
        return remote(block, block, p2_ss.at[i - 1], p2_rs.at[i - 1], at_tsg((tsg + i) % 8))

    mygain = pl.ds(pl.multiple_of(me * 24, 8), 24)

    def p3_copy(i):
        p = (me + i) % SRC
        block = acc2.at[mygain, pl.ds(128, 128)]
        return remote(block, block, p3_ss.at[i - 1], p3_rs.at[i - 1], at_gx(p // 4, p % 4))

    def router_rows():
        others(own_d, lambda d: p1_arrival(d).wait_recv())
        for n in range(D // 128):
            rows = [acc2[e * 48 + n : e * 48 + n + 1, 0:128] for e in range(PEERS)]
            c, o = n * 128 // CW, 256 + n * 128 % CW
            at = pl.ds(pl.multiple_of(c * EXPERTS + tsg * 8, 8), 8)
            acc2[at, o : o + 128] = jnp.concatenate(rows, axis=0)
        tot = acc2[24:48, 0:128]
        for e in range(1, PEERS):
            tot = tot + acc2[e * 48 + 24 : (e + 1) * 48, 0:128]
        acc2[mygain, 128:256] = tot
        for i in range(1, 8):
            for c in range(NC):
                p2_copy(i, c).start()
        for i in range(1, SRC):
            p3_copy(i).start()

    pl.semaphore_wait(free_sem.at[0], 6)


    def z_line(c, i):
        gg = (g + i) % 4
        return remote(
            send.at[c, pl.ds(pl.multiple_of(gg * 4 * TOK, 4 * TOK), 4 * TOK)],
            xall.at[NC + c, pl.ds((i - 1) * 4 * TOK, 4 * TOK)],
            z_ss.at[c, i - 1],
            z_rs.at[c, i - 1],
            at_gx(gg, x),
        )

    def z_piece(c, i, k):
        xx = (x + i) % 4
        return remote(
            send.at[c, pl.ds(pl.multiple_of((k * 4 + xx) * TOK, TOK), TOK)],
            xall.at[NC + c, pl.ds(pl.multiple_of((i - 1) * 4 * TOK + k * TOK, TOK), TOK)],
            z_ss.at[c, i - 1],
            z_rs.at[c, i - 1],
            at_gx(g, xx),
        )

    def x_copy(c, i, along_x):
        xx, gg = ((x + i) % 4, g) if along_x else (x, (g + i) % 4)
        return remote(
            send.at[c, pl.ds(pl.multiple_of((gg * 4 + xx) * TOK, TOK), TOK)],
            xall.at[NC + c, pl.ds(12 * TOK + (i - 1) * TOK, TOK)],
            x_ss.at[c, i - 1],
            x_rs.at[c, i - 1],
            at_gx(gg, xx),
        )

    def comb_body(c):
        others(own_d, lambda d: ret_arrival(c, d).wait_recv())
        others(seat, lambda e: ret_copy(c, e).wait_send())
        own_ret(c).wait()

        def body(i, _):
            gg = (g + 1 + i) % 4
            rows = pl.ds(pl.multiple_of(gg * 4 * TOK, 4 * TOK), 4 * TOK)
            low = dot(da[rows, 0:KA], xall[c, 0:KA, :])
            send[c, rows, :] = (low + dot(db[rows, 0:KB], xall[c, KA:ROWS, :])).astype(BF16)

            @pl.when((i < 3) & (c >= 2))
            def _():
                z_line(c, i + 1).start()

            @pl.when(c < 2)
            def _():
                for k in (1, 3, 2):
                    z_piece(c, k, gg).start()

            return 0

        lax.fori_loop(0, 4, body, 0)

    def z_sum(c):
        for i in (1, 3, 2):
            z_line(c, i).wait_recv()

        def body(k, _):
            row = jnp.where(c >= 2, g * 4 + k, k * 4 + x) * TOK
            rows = pl.ds(pl.multiple_of(row, TOK), TOK)
            tot = send[c, rows, :].astype(F32)
            for i in range(3):
                part = pl.ds(pl.multiple_of((i * 4 + k) * TOK, TOK), TOK)
                tot = tot + xall[NC + c, part, :].astype(F32)
            send[c, rows, :] = tot.astype(BF16)
            return 0

        lax.fori_loop(0, 4, body, 0)

        @pl.when(c >= 2)
        def _():
            for i in (1, 3, 2):
                x_copy(c, i, True).start()

        @pl.when(c < 2)
        def _():
            for i in (1, 3, 2):
                x_copy(c, i, False).start()

    def own_router():
        pad = jnp.concatenate([dzs[...], jnp.zeros((64, 128), F32)], axis=0)
        acc1[0:128, 0:128] = jnp.transpose(pad)
        dz_own = acc1[pl.ds(pl.multiple_of(dp * TOK, TOK), TOK), 0:EXPERTS]
        hi, lo = split(dz_own)
        both = dot(jnp.concatenate([hi, lo], axis=0), order()).astype(BF16)
        for c in range(NC):
            cols = slice(c * CW, (c + 1) * CW)
            two = dot(both, rw_in[:, cols])
            gx_out[:, cols] = two[0:TOK] + two[TOK : 2 * TOK]

    wgrad_body(0, 0)
    comb_body(0)
    slots_out()
    wgrad_body(1, 0)
    comb_body(1)
    z_sum(0)
    wgrad_body(2, 0)
    comb_body(2)
    z_sum(1)
    wgrad_body(3, 0)
    comb_body(3)
    z_sum(2)
    wgrad_body(4, 0)
    router_row()
    comb_body(4)
    z_sum(3)
    router_rows()
    own_router()
    z_sum(4)

    wide = tok[...].astype(F32)
    inv = lax.rsqrt(jnp.mean(wide * wide, axis=1, keepdims=True) + 1e-06)

    for i in range(1, 8):
        p2_all(i).wait_recv()
    for i in range(1, SRC):
        p3_copy(i).wait_recv()
    tot = acc2[0:24, 128:256]
    for p in range(1, SRC):
        tot = tot + acc2[p * 24 : (p + 1) * 24, 128:256]
    thrice = jnp.concatenate([order()] * 3, axis=1)
    for c in range(NC):
        rest = acc2[c * EXPERTS : (c + 1) * EXPERTS, 256 : 256 + CW]
        parts = []
        for _ in range(3):
            hi, rest = split32(rest)
            parts.append(hi)
        gr_out[:, c * CW : (c + 1) * CW] = dot(thrice, jnp.concatenate(parts, axis=0))
    for n in range(D // 128):
        cols = slice(n * 128, (n + 1) * 128)
        along = jnp.sum(gr_out[:, cols] * rw_in[:, cols].astype(F32), axis=0, keepdims=True)
        gn_out[:, cols] = (along + tot[n : n + 1, :]) / gain[:, cols]

    for c in range(NC):
        cols = slice(c * CW, (c + 1) * CW)
        du = gx_out[:, cols]
        for i in (1, 3, 2):
            x_copy(c, i, True).wait_recv()
        du = du + send[c, pl.ds(mine, TOK), :].astype(F32)
        for i in range(3):
            du = du + xall[NC + c, (12 + i) * TOK : (13 + i) * TOK, :].astype(F32)
        gx_out[:, cols] = du * gain[:, cols]
    v = wide * inv
    scaled = gx_out[...]
    gx_out[...] = inv * scaled - v * inv * jnp.mean(v * scaled, axis=1, keepdims=True)

    def drain2(c, _):
        for i in (1, 3, 2):
            z_line(c, i).wait_send()
            x_copy(c, i, True).wait_send()
        for i in range(3):
            out_copy(i, c).wait()
        return 0

    lax.fori_loop(0, NC, drain2, 0)
    for i in range(1, 8):
        rt_copy(i).wait_send()
        zb_copy(i).wait_send()
        p2_all(i).wait_send()
    others(own_d, lambda d: zs_copy(d).wait_send())
    others(seat, lambda e: dg_copy(e).wait_send())
    others(seat, lambda e: p1_copy(e).wait_send())
    for i in range(1, SRC):
        p3_copy(i).wait_send()
        dt_copy(i).wait_send()


def call(tok, dy, rt, gain, rwt, wg, wu, wd):
    vmem = pl.BlockSpec(memory_space=pltpu.VMEM)
    hbm = pl.BlockSpec(memory_space=pl.ANY)
    V = pltpu.VMEM
    S = pltpu.SemaphoreType.DMA
    weight = jax.ShapeDtypeStruct((SH, D), BF16)
    return pl.pallas_call(
        kernel,
        out_shape=(
            jax.ShapeDtypeStruct((TOK, D), F32),
            jax.ShapeDtypeStruct((EXPERTS, D), F32),
            jax.ShapeDtypeStruct((1, D), F32),
            weight, weight, weight,
        ),
        in_specs=[vmem] * 5 + [hbm] * 3,
        out_specs=(vmem, vmem, vmem, hbm, hbm, hbm),
        scratch_shapes=[
            V((2 * NC, ROWS, CW), BF16),
            V((2 * NC, ROWS, CW), BF16),
            V((NC, ROWS, CW), BF16),
            V((NC, SH, CW), BF16), V((NC, SH, CW), BF16), V((NC, SH, CW), BF16),
            V((SH, ROWS), F32), V((SH, ROWS), F32),
            V((SH, ROWS), BF16), V((SH, ROWS), BF16), V((SH, ROWS), BF16),
            V((ROWS, SH), BF16), V((ROWS, SH), BF16),
            V((ROWS, ALL), BF16),
            V((8, 8, 128), jnp.int32),
            V((EXPERTS, ALL), F32),
            V((16, ALL), jnp.int32),
            V((8, 8, 256), F32), V((8, 8, 256), F32),
            V((8, 8, 256), F32), V((8, 8, 256), F32),
            V((8, 8, 128), F32), V((8, 8, 128), F32), V((SRC, 8, 128), F32),
            V((8, ROWS), F32), V((8, ROWS), F32),
            V((1, ALL), F32), V((EXPERTS, 128), F32),
            V((NC, 8, CW), F32), V((8, 8, 256), F32), V((48, 128), F32), V((8, ALL), F32), V((256, 128), F32), V((NC, 8, CW), F32),
            S((3, NC)), S((3, NC)), S((2 * NC,)),
            S((7,)), S((7,)),
            S((2 * NC, 3)), S((2 * NC, 3)), S((2 * NC, 2)), S((2 * NC, 2)), S((2 * NC, 2)), S((2 * NC, 2)),
            S((2 * NC, 8)), S((2 * NC, 8)),
            S((8,)), S((8,)), S((8,)), S((8,)),
            S((15,)), S((15,)),
            S((NC, 8)), S((NC, 8)),
            S((NC, 3)), S((NC, 3)), S((NC, 3)), S((NC, 3)),
            S((7,)), S((7,)), S((8,)), S((8,)), S((8,)), S((8,)),
            S((7,)), S((7,)), S((15,)), S((15,)),
            pltpu.SemaphoreType.REGULAR((1,)),
        ],
        compiler_params=pltpu.CompilerParams(
            collective_id=0, has_side_effects=True, vmem_limit_bytes=VMEM_LIMIT
        ),
    )(tok, dy, rt, gain, rwt, wg, wu, wd)


VMEM_LIMIT = 65472 * 1024


def local(tokens, out_grad, routes, norm_gain, router_w, w_gate, w_up, w_down):
    core = lax.axis_index("ep") % 2
    ids = routes[0].T
    turned = (ids // 32) * 32 + (ids // 2 % 4) * 8 + (ids // 8 % 4) * 2 + ids % 2
    rt = jnp.pad(jnp.where(core == 0, ids, turned), ((0, 2), (0, 0)), constant_values=-1)
    gain = norm_gain.astype(F32)[None]

    gx, grt, gn, gg, gu, gd = call(
        tokens[0], out_grad[0], rt, gain, router_w.T, w_gate[0], w_up[0], w_down[0]
    )
    return (gx[None], gg[None], gu[None], gd[None], grt.T, gn[0])


def solution(mesh):
    split3 = P(("ts", "ep"), "dp", None)
    return jax.shard_map(
        local,
        mesh=mesh,
        in_specs=(split3, split3, P(("ts", "ep"), None, None), P(), P(), split3, split3, split3),
        out_specs=(split3, split3, split3, split3, P(), P()),
        check_vma=False,
    )
```
